256 devices in a mesh: dp: 16 (over y, x), tensor: 16 (over z, core).
Axes of the slice: x: 4, y: 4, z: 8, core: 2. Of those that a mesh axis runs over, the one named last changes fastest.
Arguments:
- tokens: bfloat16 [1024, 8192], P('tensor', 'dp'), may hold values from -6 to 6
- gate_weight: bfloat16 [8192, 14336], P('dp', 'tensor'), may hold values from -0.0625 to 0.0625
- up_weight: bfloat16 [8192, 14336], P('dp', 'tensor'), may hold values from -0.0625 to 0.0625
- down_weight: bfloat16 [14336, 8192], P('tensor', 'dp'), may hold values from -0.046875 to 0.046875
- out_grad: bfloat16 [1024, 8192], P('tensor', 'dp'), may hold values from -6 to 6
Outputs:
- ffn_output: bfloat16 [1024, 8192], P('tensor', 'dp')
- input_grad: bfloat16 [1024, 8192], P('tensor', 'dp')
- gate_weight_grad: float32 [8192, 14336], P('dp', 'tensor')
- up_weight_grad: float32 [8192, 14336], P('dp', 'tensor')
- down_weight_grad: float32 [14336, 8192], P('tensor', 'dp')
The draws below stay inside these ranges and needn't reach their ends.
All inputs are finite; a program needn't handle non-finite values.
Results may differ from the reference program's by a relative error of at most 0.0049.
Values may be sent and summed in bfloat16 or wider, within the bound.
No kernel may reach another device: no remote copies, remote signals or barrier semaphores. Data moves between devices by JAX's collectives and lax.ppermute only.
A program may use at most 128 MiB of HBM per device.

```python
import math
import jax
import jax.numpy as jnp
from jax import lax

D = 8192
FF = 14336
TOKENS = 1024


def block_levels(rng, dims, pieces, low, largest):
    factor_of = 1.0
    for position, blocks in pieces:
        heights = jax.random.uniform(jax.random.fold_in(jax.random.fold_in(rng, 6), position), (blocks,), jnp.float32, low / len(pieces), largest / len(pieces))
        factor_of = factor_of * jnp.repeat(jnp.exp(heights), dims[position] // blocks).reshape((-1,) + (1,) * (len(dims) - 1 - position))
    return factor_of


def centred(own_key, dims, scale, limit, cuts=(), kind=jnp.bfloat16):
    entries = jax.random.normal(own_key, dims, jnp.float32) * scale
    if len(cuts) > 0:
        entries = block_levels(own_key, dims, cuts, -0.22, 0.18) * entries
    return jnp.clip(entries, min=-limit, max=limit).astype(kind)


def setup_inputs(seed: int = 0) -> dict:
    seeds = jax.random.split(jax.random.key(seed), 6)
    return {
        "tokens": centred(seeds[0], (TOKENS, D), 1.0, 6.0, ((0, 16), (1, 16))),
        "gate_weight": centred(seeds[1], (D, FF), D ** -0.5, 0.0625, ((0, 16), (1, 16))),
        "up_weight": centred(seeds[2], (D, FF), D ** -0.5, 0.0625, ((0, 16), (1, 16))),
        "down_weight": centred(seeds[3], (FF, D), FF ** -0.5, 0.046875, ((0, 16), (1, 16))),
        "out_grad": centred(seeds[4], (TOKENS, D), 1.0, 6.0, ((0, 16), (1, 16))),
    }


def reference(tokens, gate_weight, up_weight, down_weight, out_grad):
    gate = jnp.dot(tokens, gate_weight, preferred_element_type=jnp.float32)
    up = jnp.dot(tokens, up_weight, preferred_element_type=jnp.float32)
    sigmoid_gate = jax.nn.sigmoid(gate)
    activated = gate * sigmoid_gate
    hidden = (activated * up).astype(jnp.bfloat16)
    ffn_output = jnp.dot(hidden, down_weight, preferred_element_type=jnp.float32).astype(jnp.bfloat16)
    hidden_grad = lax.dot_general(out_grad, down_weight, (((1,), (1,)), ((), ())), preferred_element_type=jnp.float32)
    up_grad = (hidden_grad * activated).astype(jnp.bfloat16)
    gate_grad = (hidden_grad * up * sigmoid_gate * (1.0 + gate * (1.0 - sigmoid_gate))).astype(jnp.bfloat16)
    input_grad = lax.dot_general(gate_grad, gate_weight, (((1,), (1,)), ((), ())), preferred_element_type=jnp.float32)
    input_grad = input_grad + lax.dot_general(up_grad, up_weight, (((1,), (1,)), ((), ())), preferred_element_type=jnp.float32)
    factor = 1.0 / math.sqrt(TOKENS)
    gate_weight_grad = lax.dot_general(tokens, gate_grad, (((0,), (0,)), ((), ())), preferred_element_type=jnp.float32) * factor
    up_weight_grad = lax.dot_general(tokens, up_grad, (((0,), (0,)), ((), ())), preferred_element_type=jnp.float32) * factor
    down_weight_grad = lax.dot_general(hidden, out_grad, (((0,), (0,)), ((), ())), preferred_element_type=jnp.float32) * factor
    return (ffn_output, input_grad.astype(jnp.bfloat16), gate_weight_grad, up_weight_grad, down_weight_grad)
```

```python
import math

import jax
import jax.numpy as jnp
from jax import lax
from jax.experimental import pallas as pl
from jax.experimental.pallas import tpu as pltpu
from jax.sharding import PartitionSpec as P

MIB = 1024 * 1024
BF16 = jnp.bfloat16
F32 = jnp.float32


def dot(a, b, contract):
    return lax.dot_general(a, b, ((contract[:1], contract[1:]), ((), ())), preferred_element_type=F32)


def params():
    return pltpu.CompilerParams(vmem_limit_bytes=48 * MIB)


def project(both, gate_weight, up_weight, down_weight):
    rows, width = both.shape[0], both.shape[1] // 2
    hidden = gate_weight.shape[1]
    tile = 256

    def kernel(both_ref, gate_ref, up_ref, down_ref, out_ref):
        tokens, grads = both_ref[:, :width], both_ref[:, width:]
        out_ref[:, :hidden] = dot(tokens, gate_ref[...], (1, 0)).astype(BF16)
        out_ref[:, hidden : 2 * hidden] = dot(tokens, up_ref[...], (1, 0)).astype(BF16)
        out_ref[:, 2 * hidden :] = dot(grads, down_ref[...], (1, 1)).astype(BF16)

    whole = lambda a: pl.BlockSpec(a.shape, lambda i: (0, 0))
    return pl.pallas_call(
        kernel,
        grid=(rows // tile,),
        in_specs=[
            pl.BlockSpec((tile, 2 * width), lambda i: (i, 0)),
            whole(gate_weight),
            whole(up_weight),
            whole(down_weight),
        ],
        out_specs=pl.BlockSpec((tile, 3 * hidden), lambda i: (i, 0)),
        out_shape=jax.ShapeDtypeStruct((rows, 3 * hidden), BF16),
        compiler_params=params(),
    )(both, gate_weight, up_weight, down_weight)


def activate(parts):
    count, rows, columns = parts.shape
    hidden = columns // 3
    tile = 16

    def kernel(parts_ref, out_ref):
        def total(k):
            return jnp.sum(parts_ref[:, :, k * hidden : (k + 1) * hidden].astype(F32), axis=0)

        gate, up, hidden_grad = total(0), total(1), total(2)
        s = jax.nn.sigmoid(gate)
        activated = gate * s
        out_ref[:, :hidden] = (activated * up).astype(BF16)
        out_ref[:, hidden : 2 * hidden] = (hidden_grad * up * s * (1.0 + gate * (1.0 - s))).astype(BF16)
        out_ref[:, 2 * hidden :] = (hidden_grad * activated).astype(BF16)

    return pl.pallas_call(
        kernel,
        grid=(rows // tile,),
        in_specs=[pl.BlockSpec((count, tile, columns), lambda i: (0, i, 0))],
        out_specs=pl.BlockSpec((tile, columns), lambda i: (i, 0)),
        out_shape=jax.ShapeDtypeStruct((rows, columns), BF16),
        compiler_params=params(),
    )(parts)


def back(acts, gate_weight, up_weight, down_weight):
    rows, hidden, width = acts.shape[0], gate_weight.shape[1], gate_weight.shape[0]
    tile = 256

    def kernel(acts_ref, gate_ref, up_ref, down_ref, out_ref):
        out_ref[:, :width] = dot(acts_ref[:, :hidden], down_ref[...], (1, 0))
        out_ref[:, width:] = dot(acts_ref[:, hidden : 2 * hidden], gate_ref[...], (1, 1)) + dot(
            acts_ref[:, 2 * hidden :], up_ref[...], (1, 1)
        )

    whole = lambda a: pl.BlockSpec(a.shape, lambda i: (0, 0))
    return pl.pallas_call(
        kernel,
        grid=(rows // tile,),
        in_specs=[
            pl.BlockSpec((tile, 3 * hidden), lambda i: (i, 0)),
            whole(gate_weight),
            whole(up_weight),
            whole(down_weight),
        ],
        out_specs=pl.BlockSpec((tile, 2 * width), lambda i: (i, 0)),
        out_shape=jax.ShapeDtypeStruct((rows, 2 * width), F32),
        compiler_params=params(),
    )(acts, gate_weight, up_weight, down_weight)


def weight_grads(both, acts, factor):
    rows, width, hidden = both.shape[0], both.shape[1] // 2, acts.shape[1] // 3

    def kernel(both_ref, acts_ref, gate_ref, up_ref, down_ref):
        tokens, grads = both_ref[:, :width], both_ref[:, width:]
        gate_ref[...] = dot(tokens, acts_ref[:, hidden : 2 * hidden], (0, 0)) * factor
        up_ref[...] = dot(tokens, acts_ref[:, 2 * hidden :], (0, 0)) * factor
        down_ref[...] = dot(acts_ref[:, :hidden], grads, (0, 0)) * factor

    return pl.pallas_call(
        kernel,
        out_shape=[
            jax.ShapeDtypeStruct((width, hidden), F32),
            jax.ShapeDtypeStruct((width, hidden), F32),
            jax.ShapeDtypeStruct((hidden, width), F32),
        ],
        compiler_params=params(),
    )(both, acts)


def body(tokens, gate_weight, up_weight, down_weight, out_grad):
    shard, width = tokens.shape
    tensor = lax.axis_size("tensor")
    dp = lax.axis_size("dp")
    rows = shard * tensor
    core = lax.axis_index("tensor") % 2
    both = lax.all_gather(jnp.concatenate([tokens, out_grad], 1), "tensor", axis=0, tiled=True)
    both = both.reshape(tensor // 2, 2, shard, 2 * width).transpose(1, 0, 2, 3).reshape(rows, 2 * width)
    partials = project(both, gate_weight, up_weight, down_weight)
    parts = lax.all_to_all(partials, "dp", 0, 0, tiled=True)
    acts = activate(parts.reshape(dp, rows // dp, parts.shape[1]))
    acts = lax.all_gather(acts, "dp", axis=0, tiled=True)
    sums = back(acts, gate_weight, up_weight, down_weight)
    half = rows // 2
    mine = lax.dynamic_slice_in_dim(sums, core * half, half, 0)
    other = lax.dynamic_slice_in_dim(sums, (1 - core) * half, half, 0)
    other = lax.ppermute(other, "tensor", [(i, i ^ 1) for i in range(tensor)])
    groups = [[z * 2 + c for z in range(tensor // 2)] for c in range(2)]
    result = lax.psum_scatter(mine + other, "tensor", scatter_dimension=0, tiled=True, axis_index_groups=groups).astype(BF16)
    grads = weight_grads(both, acts, 1.0 / math.sqrt(rows))
    return (result[:, :width], result[:, width:], *grads)


def solution(mesh):
    return jax.shard_map(
        body,
        mesh=mesh,
        in_specs=(
            P("tensor", "dp"),
            P("dp", "tensor"),
            P("dp", "tensor"),
            P("tensor", "dp"),
            P("tensor", "dp"),
        ),
        out_specs=(
            P("tensor", "dp"),
            P("tensor", "dp"),
            P("dp", "tensor"),
            P("dp", "tensor"),
            P("tensor", "dp"),
        ),
        check_vma=False,
    )
```

```python
import functools
import math

import jax
import jax.numpy as jnp
from jax import lax
from jax.experimental import pallas as pl
from jax.experimental.pallas import tpu as pltpu
from jax.sharding import PartitionSpec as P

MIB = 1024 * 1024
BF16 = jnp.bfloat16
F32 = jnp.float32
BOTH = ("dp", "tensor")
RING = 4
DEPTH = 8


def dot(a, b, contract):
    return lax.dot_general(a, b, ((contract[:1], contract[1:]), ((), ())), preferred_element_type=F32)


def place():
    dp, tensor = lax.axis_index("dp"), lax.axis_index("tensor")
    y, x, z, core = dp // RING, dp % RING, tensor // 2, tensor % 2
    return jnp.where(core == 0, x, y), jnp.where(core == 0, y, x), z, core


def tile_at(i, j):
    p, q, z, core = place()
    tile = RING * ((p + i) % RING) + (q + j) % RING
    return (tile % 2) ^ core, tile // 2, (tile // 2 - z + DEPTH) % DEPTH


def call(kernel, out, *args, flops=0):
    outs = out if isinstance(out, list) else [out]
    size = sum(a.size * a.dtype.itemsize for a in (*args, *outs))
    return pl.pallas_call(
        kernel,
        out_shape=out,
        compiler_params=pltpu.CompilerParams(vmem_limit_bytes=48 * MIB),
        cost_estimate=pl.CostEstimate(flops=flops, bytes_accessed=size, transcendentals=0),
    )(*args)


def shape(dims, dtype):
    return jax.ShapeDtypeStruct(dims, dtype)


def along(first, k):
    pairs = []
    for y in range(RING):
        for x in range(RING):
            for z in range(DEPTH):
                for core in range(2):
                    if (core == 0) == first:
                        to = (y, (x + k) % RING)
                    else:
                        to = ((y + k) % RING, x)
                    t = z * 2 + core
                    pairs.append(((y * RING + x) * 2 * DEPTH + t, (to[0] * RING + to[1]) * 2 * DEPTH + t))
    return pairs


def send_p(a, k):
    return lax.ppermute(a, BOTH, along(True, k % RING))


def send_q(a, k):
    return lax.ppermute(a, BOTH, along(False, k % RING))


def send_z(a, k):
    return lax.ppermute(a, "tensor", [(z * 2 + c, (z + k) % DEPTH * 2 + c) for z in range(DEPTH) for c in range(2)])


def send_core(a):
    return lax.ppermute(a, "tensor", [(i, i ^ 1) for i in range(2 * DEPTH)])


ORDER = (2, 1, 3)


def token_block(mine, other, i):
    tiles = []
    for j in range(RING):
        foreign, _, near = tile_at(i, j)
        tiles.append(jnp.where(foreign == 0, mine[near], other[near]))
    return jnp.concatenate(tiles, 0)


def grad_block(grads, i):
    tiles = []
    for j in range(RING):
        foreign, z, _ = tile_at(i, j)
        tiles.append(grads[2 * z + (foreign ^ place()[3])])
    return jnp.concatenate(tiles, 0)


def project(mine, other, gate_weight, up_weight, i, dtype):
    width, hidden = gate_weight.shape
    rows = RING * mine.shape[1]

    def kernel(mine_ref, other_ref, gate_ref, up_ref, out_ref):
        block = token_block(mine_ref, other_ref, i)
        out_ref[:, :hidden] = dot(block, gate_ref[...], (1, 0)).astype(dtype)
        out_ref[:, hidden:] = dot(block, up_ref[...], (1, 0)).astype(dtype)

    return call(
        kernel, shape((rows, 2 * hidden), dtype), mine, other, gate_weight, up_weight, flops=4 * rows * width * hidden
    )


def project_grad(grads, down_weight, i, dtype):
    hidden, width = down_weight.shape
    rows = RING * grads.shape[1]

    def kernel(grads_ref, down_ref, out_ref):
        out_ref[...] = dot(grad_block(grads_ref, i), down_ref[...], (1, 1)).astype(dtype)

    return call(kernel, shape((rows, hidden), dtype), grads, down_weight, flops=2 * rows * width * hidden)


def add_blocks(own, parts):
    rows, columns = own.shape
    tile = rows // RING

    def kernel(own_ref, a_ref, b_ref, c_ref, *outs):
        for j, out in enumerate(outs):
            at = pl.ds(j * tile, tile)
            out[...] = own_ref[at] + (a_ref[at].astype(F32) + b_ref[at].astype(F32) + c_ref[at].astype(F32))

    return call(kernel, [shape((tile, columns), F32)] * RING, own, *parts)


def reduce_dp(blocks):
    parts = [send_p(blocks[i], i) for i in ORDER]
    tiles = add_blocks(blocks[0], parts)
    return [tiles[0]] + [send_q(tiles[j], j) for j in ORDER]


def activate(terms):
    rows, columns = terms[0].shape
    hidden = columns // 2

    def kernel(a, b, c, d, hidden_ref, up_factor, gate_factor):
        def total(at):
            return (a[:, at] + b[:, at]) + (c[:, at] + d[:, at])

        gate, up = total(pl.ds(0, hidden)), total(pl.ds(hidden, hidden))
        s = jax.nn.sigmoid(gate)
        activated = gate * s
        hidden_ref[...] = (activated * up).astype(BF16)
        up_factor[...] = activated
        gate_factor[...] = up * s * (1.0 + gate * (1.0 - s))

    return call(
        kernel, [shape((rows, hidden), BF16), shape((rows, hidden), F32), shape((rows, hidden), F32)], *terms
    )


def activate_grad(terms, up_factor, gate_factor):
    rows, hidden = up_factor.shape

    def kernel(a, b, c, d, up_ref, gate_ref, out_ref):
        hidden_grad = (a[...] + b[...]) + (c[...] + d[...])
        out_ref[:, :hidden] = (hidden_grad * gate_ref[...]).astype(BF16)
        out_ref[:, hidden:] = (hidden_grad * up_ref[...]).astype(BF16)

    return call(kernel, shape((rows, 2 * hidden), BF16), *terms, up_factor, gate_factor)


def gather_dp(tile):
    near = [tile] + [send_q(tile, -j) for j in (1, 2, 3)]
    block = jnp.concatenate(near, 0)
    return [block] + [send_p(block, -i) for i in (1, 2, 3)]


def store_tiles(mine, other, i, result, relative):
    tile = mine.shape[1]
    for j in range(RING):
        foreign, z, near = tile_at(i, j)
        at = near if relative else z
        part = result[j * tile : (j + 1) * tile]

        @pl.when(foreign == 0)
        def _():
            mine[at] = part

        @pl.when(foreign == 1)
        def _():
            other[at] = part


def back_hidden(blocks, down_weight):
    hidden, width = down_weight.shape
    rows = blocks[0].shape[0]

    def kernel(a, b, c, d, down_ref, mine, other):
        for i, block in enumerate((a, b, c, d)):
            store_tiles(mine, other, i, dot(block[...], down_ref[...], (1, 0)), False)

    half = shape((DEPTH, rows // RING, width), F32)
    return call(kernel, [half, half], *blocks, down_weight, flops=2 * RING * rows * width * hidden)


def back_grads(blocks, gate_weight, up_weight):
    width, hidden = gate_weight.shape
    rows = blocks[0].shape[0]

    def kernel(a, b, c, d, gate_ref, up_ref, mine, other):
        for i, block in enumerate((a, b, c, d)):
            result = dot(block[:, :hidden], gate_ref[...], (1, 1)) + dot(block[:, hidden:], up_ref[...], (1, 1))
            store_tiles(mine, other, i, result, True)

    half = shape((DEPTH, rows // RING, width), F32)
    return call(kernel, [half, half], *blocks, gate_weight, up_weight, flops=4 * RING * rows * width * hidden)


def scatter_z(mine, arrived):
    depth, rows, width = mine.shape

    def split(mine_ref, arrived_ref, *outs):
        for k, out in enumerate(outs):
            out[...] = (mine_ref[k] + arrived_ref[k]).astype(out.dtype)

    tiles = call(split, [shape((rows, width), F32 if k == 0 else BF16) for k in range(depth)], mine, arrived)
    terms = [tiles[0]] + [send_z(tiles[k], k) for k in (4, 3, 5, 2, 6, 1, 7)]

    def add(*refs):
        total = refs[0][...]
        for ref in refs[1:-1]:
            total += ref[...].astype(F32)
        refs[-1][...] = total.astype(BF16)

    return call(add, shape((rows, width), BF16), *terms)


def hidden_weight_grad(blocks, grads, factor):
    rows, hidden = blocks[0].shape
    width = grads.shape[2]

    def kernel(a, b, c, d, grads_ref, out_ref):
        for i, block in enumerate((a, b, c, d)):
            part = dot(block[...], grad_block(grads_ref, i), (0, 0)) * factor
            if i == 0:
                out_ref[...] = part
            else:
                out_ref[...] += part

    return call(
        kernel, shape((hidden, width), F32), *blocks, grads, flops=2 * RING * rows * width * hidden
    )


def token_weight_grads(blocks, mine, other, factor):
    rows, hidden = blocks[0].shape[0], blocks[0].shape[1] // 2
    width = mine.shape[2]

    def kernel(a, b, c, d, mine_ref, other_ref, gate_ref, up_ref):
        for i, block in enumerate((a, b, c, d)):
            tokens = token_block(mine_ref, other_ref, i)
            gate = dot(tokens, block[:, :hidden], (0, 0)) * factor
            up = dot(tokens, block[:, hidden:], (0, 0)) * factor
            if i == 0:
                gate_ref[...] = gate
                up_ref[...] = up
            else:
                gate_ref[...] += gate
                up_ref[...] += up

    out = shape((width, hidden), F32)
    return call(kernel, [out, out], *blocks, mine, other, flops=4 * RING * rows * width * hidden)


def body(tokens, gate_weight, up_weight, down_weight, out_grad):
    shard, width = tokens.shape
    rows = shard * 2 * DEPTH
    factor = 1.0 / math.sqrt(rows)

    grads = lax.all_gather(out_grad, "tensor", axis=0)
    arrived = {k: send_z(tokens, -k) for k in (4, 3, 5, 2, 6, 1, 7)}
    mine = jnp.stack([tokens] + [arrived[k] for k in range(1, DEPTH)])
    other = send_core(mine)

    terms = reduce_dp(
        {i: project(mine, other, gate_weight, up_weight, i, BF16 if i else F32) for i in (*ORDER, 0)}
    )
    hidden, up_factor, gate_factor = activate(terms)
    grad_terms = reduce_dp({i: project_grad(grads, down_weight, i, BF16 if i else F32) for i in (*ORDER, 0)})
    hidden_blocks = gather_dp(hidden)
    grad_blocks = gather_dp(activate_grad(grad_terms, up_factor, gate_factor))

    keep, give = back_hidden(hidden_blocks, down_weight)
    half = (keep + send_core(give)).reshape(rows // 2, width)
    groups = [[z * 2 + c for z in range(DEPTH)] for c in range(2)]
    ffn_output = lax.psum_scatter(
        half, "tensor", scatter_dimension=0, tiled=True, axis_index_groups=groups
    ).astype(BF16)
    down_weight_grad = hidden_weight_grad(hidden_blocks, grads, factor)

    keep, give = back_grads(grad_blocks, gate_weight, up_weight)
    input_grad = scatter_z(keep, send_core(give))
    gate_weight_grad, up_weight_grad = token_weight_grads(grad_blocks, mine, other, factor)
    return ffn_output, input_grad, gate_weight_grad, up_weight_grad, down_weight_grad


def solution(mesh):
    return jax.shard_map(
        body,
        mesh=mesh,
        in_specs=(
            P("tensor", "dp"),
            P("dp", "tensor"),
            P("dp", "tensor"),
            P("tensor", "dp"),
            P("tensor", "dp"),
        ),
        out_specs=(
            P("tensor", "dp"),
            P("tensor", "dp"),
            P("dp", "tensor"),
            P("dp", "tensor"),
            P("tensor", "dp"),
        ),
        check_vma=False,
    )
```

```python
import functools
import math

import jax
import jax.numpy as jnp
from jax import lax
from jax.experimental import pallas as pl
from jax.experimental.pallas import tpu as pltpu
from jax.sharding import PartitionSpec as P

MIB = 1024 * 1024
BF16 = jnp.bfloat16
F32 = jnp.float32
BOTH = ("dp", "tensor")
RING = 4
DEPTH = 8


def dot(a, b, contract):
    return lax.dot_general(a, b, ((contract[:1], contract[1:]), ((), ())), preferred_element_type=F32)


def place():
    dp, tensor = lax.axis_index("dp"), lax.axis_index("tensor")
    y, x, z, core = dp // RING, dp % RING, tensor // 2, tensor % 2
    return jnp.where(core == 0, x, y), jnp.where(core == 0, y, x), z, core


def tile_at(i, j):
    p, q, z, core = place()
    tile = RING * ((p + i) % RING) + (q + j) % RING
    return (tile % 2) ^ core, tile // 2, (tile // 2 - z + DEPTH) % DEPTH


def call(kernel, out, *args, flops=0):
    outs = out if isinstance(out, list) else [out]
    size = sum(a.size * a.dtype.itemsize for a in (*args, *outs))
    return pl.pallas_call(
        kernel,
        out_shape=out,
        compiler_params=pltpu.CompilerParams(vmem_limit_bytes=48 * MIB),
        cost_estimate=pl.CostEstimate(flops=flops, bytes_accessed=size, transcendentals=0),
    )(*args)


def shape(dims, dtype):
    return jax.ShapeDtypeStruct(dims, dtype)


def along(first, k):
    pairs = []
    for y in range(RING):
        for x in range(RING):
            for z in range(DEPTH):
                for core in range(2):
                    if (core == 0) == first:
                        to = (y, (x + k) % RING)
                    else:
                        to = ((y + k) % RING, x)
                    t = z * 2 + core
                    pairs.append(((y * RING + x) * 2 * DEPTH + t, (to[0] * RING + to[1]) * 2 * DEPTH + t))
    return pairs


def send_p(a, k):
    return lax.ppermute(a, BOTH, along(True, k % RING))


def send_q(a, k):
    return lax.ppermute(a, BOTH, along(False, k % RING))


def send_z(a, k):
    return lax.ppermute(a, "tensor", [(z * 2 + c, (z + k) % DEPTH * 2 + c) for z in range(DEPTH) for c in range(2)])


def send_core(a):
    return lax.ppermute(a, "tensor", [(i, i ^ 1) for i in range(2 * DEPTH)])


ORDER = (2, 1, 3)


def token_block(mine, other, i, part):
    width = mine.shape[2] // 2
    columns = pl.ds(part * width, width)
    tiles = []
    for j in range(RING):
        foreign, _, near = tile_at(i, j)
        tiles.append(jnp.where(foreign == 0, mine[near, :, columns], other[near, :, columns]))
    return jnp.concatenate(tiles, 0)


def join(*tiles):
    rows, columns = tiles[0].shape

    def kernel(*refs):
        for j, ref in enumerate(refs[:-1]):
            refs[-1][pl.ds(j * rows, rows)] = ref[...]

    return call(kernel, shape((len(tiles) * rows, columns), tiles[0].dtype), *tiles)


def gather_z(a):
    arrived = {k: send_z(a, -k) for k in (4, 3, 5, 2, 6, 1, 7)}
    mine = jnp.stack([a] + [arrived[k] for k in range(1, DEPTH)])
    return mine, send_core(mine)


def project(mine, other, gate_weight, up_weight, i, dtype):
    width, hidden = gate_weight.shape
    rows = RING * mine.shape[1]

    def kernel(mine_ref, other_ref, gate_ref, up_ref, out_ref):
        block = token_block(mine_ref, other_ref, i, 0)
        out_ref[:, :hidden] = dot(block, gate_ref[...], (1, 0)).astype(dtype)
        out_ref[:, hidden:] = dot(block, up_ref[...], (1, 0)).astype(dtype)

    return call(
        kernel, shape((rows, 2 * hidden), dtype), mine, other, gate_weight, up_weight, flops=4 * rows * width * hidden
    )


def project_grad(mine, other, down_weight, i, dtype):
    hidden, width = down_weight.shape
    rows = RING * mine.shape[1]

    def kernel(mine_ref, other_ref, down_ref, out_ref):
        out_ref[...] = dot(token_block(mine_ref, other_ref, i, 1), down_ref[...], (1, 1)).astype(dtype)

    return call(kernel, shape((rows, hidden), dtype), mine, other, down_weight, flops=2 * rows * width * hidden)


def add_blocks(own, parts):
    rows, columns = own.shape
    tile = rows // RING

    def kernel(own_ref, a_ref, b_ref, c_ref, *outs):
        for j, out in enumerate(outs):
            at = pl.ds(j * tile, tile)
            out[...] = own_ref[at] + (a_ref[at].astype(F32) + b_ref[at].astype(F32) + c_ref[at].astype(F32))

    return call(kernel, [shape((tile, columns), F32)] * RING, own, *parts)


def reduce_dp(blocks):
    parts = [send_p(blocks[i], i) for i in ORDER]
    tiles = add_blocks(blocks[0], parts)
    return [tiles[0]] + [send_q(tiles[j], j) for j in ORDER]


def activate(terms):
    rows, columns = terms[0].shape
    hidden = columns // 2

    def kernel(a, b, c, d, hidden_ref, up_factor, gate_factor):
        def total(at):
            return (a[:, at] + b[:, at]) + (c[:, at] + d[:, at])

        gate, up = total(pl.ds(0, hidden)), total(pl.ds(hidden, hidden))
        s = jax.nn.sigmoid(gate)
        activated = gate * s
        hidden_ref[...] = (activated * up).astype(BF16)
        up_factor[...] = activated
        gate_factor[...] = up * s * (1.0 + gate * (1.0 - s))

    return call(
        kernel, [shape((rows, hidden), BF16), shape((rows, hidden), F32), shape((rows, hidden), F32)], *terms
    )


def activate_grad(terms, up_factor, gate_factor):
    rows, hidden = up_factor.shape

    def kernel(a, b, c, d, up_ref, gate_ref, out_ref):
        hidden_grad = (a[...] + b[...]) + (c[...] + d[...])
        out_ref[:, :hidden] = (hidden_grad * gate_ref[...]).astype(BF16)
        out_ref[:, hidden:] = (hidden_grad * up_ref[...]).astype(BF16)

    return call(kernel, shape((rows, 2 * hidden), BF16), *terms, up_factor, gate_factor)


def gather_dp(tile):
    near = [tile] + [send_q(tile, -j) for j in (1, 2, 3)]
    block = join(*near)
    return [block] + [send_p(block, -i) for i in (1, 2, 3)]


def store_tiles(mine, other, result, relative):
    tile = mine.shape[1]
    for k in range(RING * RING):
        foreign, z, near = tile_at(k // RING, k % RING)
        at = near if relative else z
        part = result[k * tile : (k + 1) * tile]

        @pl.when(foreign == 0)
        def _():
            mine[at] = part

        @pl.when(foreign == 1)
        def _():
            other[at] = part


def back_hidden(blocks, down_weight):
    hidden, width = down_weight.shape
    rows = blocks[0].shape[0]

    def kernel(a, b, c, d, down_ref, mine, other):
        blocks = jnp.concatenate([block[...] for block in (a, b, c, d)], 0)
        store_tiles(mine, other, dot(blocks, down_ref[...], (1, 0)), False)

    half = shape((DEPTH, rows // RING, width), F32)
    return call(kernel, [half, half], *blocks, down_weight, flops=2 * RING * rows * width * hidden)


def back_grads(blocks, gate_weight, up_weight):
    width, hidden = gate_weight.shape
    rows = blocks[0].shape[0]

    def kernel(a, b, c, d, gate_ref, up_ref, mine, other):
        blocks = jnp.concatenate([block[...] for block in (a, b, c, d)], 0)
        result = dot(blocks[:, :hidden], gate_ref[...], (1, 1)) + dot(blocks[:, hidden:], up_ref[...], (1, 1))
        store_tiles(mine, other, result, True)

    half = shape((DEPTH, rows // RING, width), F32)
    return call(kernel, [half, half], *blocks, gate_weight, up_weight, flops=4 * RING * rows * width * hidden)


def scatter_z(mine, arrived):
    depth, rows, width = mine.shape

    def split(mine_ref, arrived_ref, *outs):
        for k, out in enumerate(outs):
            out[...] = (mine_ref[k] + arrived_ref[k]).astype(out.dtype)

    tiles = call(split, [shape((rows, width), F32 if k == 0 else BF16) for k in range(depth)], mine, arrived)
    terms = [tiles[0]] + [send_z(tiles[k], k) for k in (4, 3, 5, 2, 6, 1, 7)]

    def add(*refs):
        total = refs[0][...]
        for ref in refs[1:-1]:
            total += ref[...].astype(F32)
        refs[-1][...] = total.astype(BF16)

    return call(add, shape((rows, width), BF16), *terms)


def hidden_weight_grad(blocks, mine, other, factor):
    rows, hidden = blocks[0].shape
    width = mine.shape[2] // 2

    def kernel(a, b, c, d, mine_ref, other_ref, out_ref):
        for i, block in enumerate((a, b, c, d)):
            part = dot(block[...], token_block(mine_ref, other_ref, i, 1), (0, 0)) * factor
            if i == 0:
                out_ref[...] = part
            else:
                out_ref[...] += part

    return call(
        kernel, shape((hidden, width), F32), *blocks, mine, other, flops=2 * RING * rows * width * hidden
    )


def token_weight_grads(blocks, mine, other, factor):
    rows, hidden = blocks[0].shape[0], blocks[0].shape[1] // 2
    width = mine.shape[2] // 2

    def kernel(a, b, c, d, mine_ref, other_ref, gate_ref, up_ref):
        for i, block in enumerate((a, b, c, d)):
            tokens = token_block(mine_ref, other_ref, i, 0)
            gate = dot(tokens, block[:, :hidden], (0, 0)) * factor
            up = dot(tokens, block[:, hidden:], (0, 0)) * factor
            if i == 0:
                gate_ref[...] = gate
                up_ref[...] = up
            else:
                gate_ref[...] += gate
                up_ref[...] += up

    out = shape((width, hidden), F32)
    return call(kernel, [out, out], *blocks, mine, other, flops=4 * RING * rows * width * hidden)


def body(tokens, gate_weight, up_weight, down_weight, out_grad):
    shard, width = tokens.shape
    rows = shard * 2 * DEPTH
    factor = 1.0 / math.sqrt(rows)

    both = gather_z(jnp.concatenate([tokens, out_grad], 1))
    blocks = {i: project(*both, gate_weight, up_weight, i, BF16 if i else F32) for i in (*ORDER, 0)}
    grad_blocks = {i: project_grad(*both, down_weight, i, BF16 if i else F32) for i in (*ORDER, 0)}

    hidden, up_factor, gate_factor = activate(reduce_dp(blocks))
    grad_terms = reduce_dp(grad_blocks)
    hidden_blocks = gather_dp(hidden)
    grad_blocks = gather_dp(activate_grad(grad_terms, up_factor, gate_factor))

    keep, give = back_hidden(hidden_blocks, down_weight)
    half = (keep + send_core(give)).reshape(rows // 2, width)
    down_weight_grad = hidden_weight_grad(hidden_blocks, *both, factor)

    grad_blocks[0], down_weight_grad, half = lax.optimization_barrier((grad_blocks[0], down_weight_grad, half))
    groups = [[z * 2 + c for z in range(DEPTH)] for c in range(2)]
    ffn_output = lax.psum_scatter(
        half, "tensor", scatter_dimension=0, tiled=True, axis_index_groups=groups
    ).astype(BF16)
    keep, give = back_grads(grad_blocks, gate_weight, up_weight)
    input_grad = scatter_z(keep, send_core(give))
    gate_weight_grad, up_weight_grad = token_weight_grads(grad_blocks, *both, factor)
    return ffn_output, input_grad, gate_weight_grad, up_weight_grad, down_weight_grad


def solution(mesh):
    return jax.shard_map(
        body,
        mesh=mesh,
        in_specs=(
            P("tensor", "dp"),
            P("dp", "tensor"),
            P("dp", "tensor"),
            P("tensor", "dp"),
            P("tensor", "dp"),
        ),
        out_specs=(
            P("tensor", "dp"),
            P("tensor", "dp"),
            P("dp", "tensor"),
            P("dp", "tensor"),
            P("tensor", "dp"),
        ),
        check_vma=False,
    )
```

```python
import functools
import math

import jax
import jax.numpy as jnp
from jax import lax
from jax.experimental import pallas as pl
from jax.experimental.pallas import tpu as pltpu
from jax.sharding import PartitionSpec as P

MIB = 1024 * 1024
BF16 = jnp.bfloat16
F32 = jnp.float32
BOTH = ("dp", "tensor")
RING = 4
DEPTH = 8


def dot(a, b, contract):
    return lax.dot_general(a, b, ((contract[:1], contract[1:]), ((), ())), preferred_element_type=F32)


def place():
    dp, tensor = lax.axis_index("dp"), lax.axis_index("tensor")
    y, x, z, core = dp // RING, dp % RING, tensor // 2, tensor % 2
    return jnp.where(core == 0, x, y), jnp.where(core == 0, y, x), z, core


def tile_at(i, j):
    p, q, _, core = place()
    tile = RING * ((p + i) % RING) + (q + j) % RING
    return (tile % 2) ^ core, tile // 2


def call(kernel, out, *args, flops=0):
    outs = out if isinstance(out, list) else [out]
    size = sum(a.size * a.dtype.itemsize for a in (*args, *outs))
    return pl.pallas_call(
        kernel,
        out_shape=out,
        compiler_params=pltpu.CompilerParams(vmem_limit_bytes=24 * MIB),
        cost_estimate=pl.CostEstimate(flops=0, bytes_accessed=0, transcendentals=0),
    )(*args)


def shape(dims, dtype):
    return jax.ShapeDtypeStruct(dims, dtype)


def along(first, k):
    pairs = []
    for y in range(RING):
        for x in range(RING):
            for z in range(DEPTH):
                for core in range(2):
                    if (core == 0) == first:
                        to = (y, (x + k) % RING)
                    else:
                        to = ((y + k) % RING, x)
                    t = z * 2 + core
                    pairs.append(((y * RING + x) * 2 * DEPTH + t, (to[0] * RING + to[1]) * 2 * DEPTH + t))
    return pairs


def send_p(a, k):
    return lax.ppermute(a, BOTH, along(True, k % RING))


def send_q(a, k):
    return lax.ppermute(a, BOTH, along(False, k % RING))


def send_core(a):
    return lax.ppermute(a, "tensor", [(i, i ^ 1) for i in range(2 * DEPTH)])


ORDER = (2, 1, 3)
CORES = [[z * 2 + c for z in range(DEPTH)] for c in range(2)]


def row_block(mine, other, i):
    tiles = []
    for j in range(RING):
        foreign, z = tile_at(i, j)
        tiles.append(jnp.where(foreign == 0, mine[z], other[z]))
    return jnp.concatenate(tiles, 0)


def join(*tiles):
    rows, columns = tiles[0].shape

    def kernel(*refs):
        for j, ref in enumerate(refs[:-1]):
            refs[-1][pl.ds(j * rows, rows)] = ref[...]

    return call(kernel, shape((len(tiles) * rows, columns), tiles[0].dtype), *tiles)


def gather_z(a):
    copies = jnp.broadcast_to(a, (DEPTH, *a.shape))
    mine = lax.all_to_all(copies, "tensor", 0, 0, tiled=True, axis_index_groups=CORES)
    return mine, send_core(mine)


def project(mine, other, gate_weight, up_weight, i, dtype):
    width, hidden = gate_weight.shape
    rows = RING * mine.shape[1]

    def kernel(mine_ref, other_ref, gate_ref, up_ref, out_ref):
        block = row_block(mine_ref, other_ref, i)
        out_ref[:, :hidden] = dot(block, gate_ref[...], (1, 0)).astype(dtype)
        out_ref[:, hidden:] = dot(block, up_ref[...], (1, 0)).astype(dtype)

    return call(
        kernel, shape((rows, 2 * hidden), dtype), mine, other, gate_weight, up_weight, flops=4 * rows * width * hidden
    )


def grad_block(grads, i):
    core = place()[3]
    tiles = []
    for j in range(RING):
        foreign, z = tile_at(i, j)
        tiles.append(grads[2 * z + (foreign ^ core)])
    return jnp.concatenate(tiles, 0)


def project_grad(grads, down_weight, i, dtype):
    hidden, width = down_weight.shape
    rows = RING * grads.shape[1]

    def kernel(grads_ref, down_ref, out_ref):
        out_ref[...] = dot(grad_block(grads_ref, i), down_ref[...], (1, 1)).astype(dtype)

    return call(kernel, shape((rows, hidden), dtype), grads, down_weight, flops=2 * rows * width * hidden)


def add_blocks(own, parts):
    rows, columns = own.shape
    tile = rows // RING

    def kernel(own_ref, a_ref, b_ref, c_ref, *outs):
        for j, out in enumerate(outs):
            at = pl.ds(j * tile, tile)
            out[...] = own_ref[at] + (a_ref[at].astype(F32) + b_ref[at].astype(F32) + c_ref[at].astype(F32))

    return call(kernel, [shape((tile, columns), F32)] * RING, own, *parts)


def spread(tiles):
    return [tiles[0]] + [send_q(tiles[j], j) for j in ORDER]


def activate(terms):
    rows, columns = terms[0].shape
    hidden = columns // 2

    def kernel(a, b, c, d, hidden_ref, up_factor, gate_factor):
        def total(at):
            return (a[:, at] + b[:, at]) + (c[:, at] + d[:, at])

        gate, up = total(pl.ds(0, hidden)), total(pl.ds(hidden, hidden))
        s = jax.nn.sigmoid(gate)
        activated = gate * s
        hidden_ref[...] = (activated * up).astype(BF16)
        up_factor[...] = activated
        gate_factor[...] = up * s * (1.0 + gate * (1.0 - s))

    return call(
        kernel, [shape((rows, hidden), BF16), shape((rows, hidden), F32), shape((rows, hidden), F32)], *terms
    )


def activate_grad(terms, up_factor, gate_factor):
    rows, hidden = up_factor.shape

    def kernel(a, b, c, d, up_ref, gate_ref, out_ref):
        hidden_grad = (a[...] + b[...]) + (c[...] + d[...])
        out_ref[:, :hidden] = (hidden_grad * gate_ref[...]).astype(BF16)
        out_ref[:, hidden:] = (hidden_grad * up_ref[...]).astype(BF16)

    return call(kernel, shape((rows, 2 * hidden), BF16), *terms, up_factor, gate_factor)


def gather_q(tile):
    return [tile] + [send_q(tile, -j) for j in range(1, RING)]


def gather_p(block):
    return [block] + [send_p(block, -i) for i in range(1, RING)]


def store_tile(mine, other, foreign, at, part):
    @pl.when(foreign == 0)
    def _():
        mine[at] = part

    @pl.when(foreign == 1)
    def _():
        other[at] = part


def store_tiles(mine, other, i, result):
    tile = mine.shape[1]
    for j in range(RING):
        store_tile(mine, other, *tile_at(i, j), result[j * tile : (j + 1) * tile])


def back(blocks, weights):
    hidden, width = weights.shape
    rows = blocks[0].shape[0]

    def kernel(a, b, c, d, weights_ref, mine, other):
        for i, block in enumerate((a, b, c, d)):
            store_tiles(mine, other, i, dot(block[...], weights_ref[...], (1, 0)))

    half = shape((DEPTH, rows // RING, width), F32)
    return call(kernel, [half, half], *blocks, weights, flops=2 * RING * rows * width * hidden)


def transposed(gate_weight, up_weight):
    width, hidden = gate_weight.shape

    def kernel(gate_ref, up_ref, out_ref):
        out_ref[:hidden] = gate_ref[...].T
        out_ref[hidden:] = up_ref[...].T

    return call(kernel, shape((2 * hidden, width), BF16), gate_weight, up_weight)


def reduce_z(mine, other, done):
    arrived = send_core(other)
    depth, rows, width = mine.shape

    def split(mine_ref, arrived_ref, own, out):
        own[...] = mine_ref[place()[2]] + arrived_ref[place()[2]]
        for k in range(depth):
            out[k] = (mine_ref[k] + arrived_ref[k]).astype(BF16)

    own, parts = call(split, [shape((rows, width), F32), shape(mine.shape, BF16)], mine, arrived)
    parts = lax.all_to_all(parts, "tensor", 0, 0, tiled=True, axis_index_groups=CORES)

    def add(own_ref, parts_ref, done_ref, out, done_out):
        total = own_ref[...]
        for k in range(depth):
            total += jnp.where(place()[2] == k, 0.0, parts_ref[k].astype(F32))
        out[...] = total.astype(BF16)
        done_out[...] = done_ref[...].astype(BF16)

    return call(add, [shape((rows, width), BF16)] * 2, own, parts, done)


def hidden_weight_grad(blocks, grads, factor):
    rows, hidden = blocks[0].shape
    width = grads.shape[2]

    def kernel(a, b, c, d, grads_ref, out_ref):
        for i, block in enumerate((a, b, c, d)):
            part = dot(block[...], grad_block(grads_ref, i), (0, 0)) * factor
            if i == 0:
                out_ref[...] = part
            else:
                out_ref[...] += part

    return call(
        kernel, shape((hidden, width), F32), *blocks, grads, flops=2 * RING * rows * width * hidden
    )


def token_weight_grads(blocks, mine, other, factor):
    rows, hidden = blocks[0].shape[0], blocks[0].shape[1] // 2
    width = mine.shape[2]

    def kernel(a, b, c, d, mine_ref, other_ref, gate_ref, up_ref):
        for i, block in enumerate((a, b, c, d)):
            tokens = row_block(mine_ref, other_ref, i)
            gate = dot(tokens, block[:, :hidden], (0, 0)) * factor
            up = dot(tokens, block[:, hidden:], (0, 0)) * factor
            if i == 0:
                gate_ref[...] = gate
                up_ref[...] = up
            else:
                gate_ref[...] += gate
                up_ref[...] += up

    out = shape((width, hidden), F32)
    return call(kernel, [out, out], *blocks, mine, other, flops=4 * RING * rows * width * hidden)


def body(tokens, gate_weight, up_weight, down_weight, out_grad):
    shard, width = tokens.shape
    rows = shard * 2 * DEPTH
    factor = 1.0 / math.sqrt(rows)

    rows_of = list(gather_z(tokens))
    grads = lax.all_gather(out_grad, "tensor", axis=0)
    blocks = {i: project(*rows_of, gate_weight, up_weight, i, BF16) for i in ORDER}
    rows_of[0], grads = lax.optimization_barrier((rows_of[0], grads))
    blocks[0] = project(*rows_of, gate_weight, up_weight, 0, F32)
    grad_blocks = {i: project_grad(grads, down_weight, i, BF16 if i else F32) for i in (*ORDER, 0)}

    blocks[0], *sent = lax.optimization_barrier((blocks[0], *(grad_blocks[i] for i in ORDER)))
    grad_blocks.update(zip(ORDER, sent))
    tiles = add_blocks(blocks[0], [send_p(blocks[i], i) for i in ORDER])
    grad_tiles = list(add_blocks(grad_blocks[0], [send_p(grad_blocks[i], i) for i in ORDER]))
    terms = spread(tiles)
    terms[0], *grad_tiles = lax.optimization_barrier((terms[0], *grad_tiles))
    hidden, up_factor, gate_factor = activate(terms)
    near = gather_q(hidden)
    grad_terms = spread(grad_tiles)
    near[0], *grad_terms = lax.optimization_barrier((near[0], *grad_terms))
    grad_near = gather_q(activate_grad(grad_terms, up_factor, gate_factor))
    hidden_blocks = gather_p(join(*near))
    grad_block = join(*grad_near)
    hidden_blocks[0], _ = lax.optimization_barrier((hidden_blocks[0], grad_block))
    grad_blocks = gather_p(grad_block)

    keep, give = back(hidden_blocks, down_weight)
    half = (keep + send_core(give)).reshape(rows // 2, width)
    down_weight_grad = hidden_weight_grad(hidden_blocks, grads, factor)
    grad_blocks[0], down_weight_grad, half = lax.optimization_barrier((grad_blocks[0], down_weight_grad, half))
    ffn_output = lax.psum_scatter(half, "tensor", scatter_dimension=0, tiled=True, axis_index_groups=CORES)
    input_grad, ffn_output = reduce_z(*back(grad_blocks, transposed(gate_weight, up_weight)), ffn_output)
    gate_weight_grad, up_weight_grad = token_weight_grads(grad_blocks, *rows_of, factor)
    return ffn_output, input_grad, gate_weight_grad, up_weight_grad, down_weight_grad


def solution(mesh):
    return jax.shard_map(
        body,
        mesh=mesh,
        in_specs=(
            P("tensor", "dp"),
            P("dp", "tensor"),
            P("dp", "tensor"),
            P("tensor", "dp"),
            P("tensor", "dp"),
        ),
        out_specs=(
            P("tensor", "dp"),
            P("tensor", "dp"),
            P("dp", "tensor"),
            P("dp", "tensor"),
            P("tensor", "dp"),
        ),
        check_vma=False,
    )
```

```python
import functools
import math

import jax
import jax.numpy as jnp
from jax import lax
from jax.experimental import pallas as pl
from jax.experimental.pallas import tpu as pltpu
from jax.sharding import PartitionSpec as P

MIB = 1024 * 1024
BF16 = jnp.bfloat16
F32 = jnp.float32
BOTH = ("dp", "tensor")
RING = 4
DEPTH = 8


def dot(a, b, contract):
    return lax.dot_general(a, b, ((contract[:1], contract[1:]), ((), ())), preferred_element_type=F32)


def place():
    dp, tensor = lax.axis_index("dp"), lax.axis_index("tensor")
    y, x, z, core = dp // RING, dp % RING, tensor // 2, tensor % 2
    return jnp.where(core == 0, x, y), jnp.where(core == 0, y, x), z, core


def tile_at(i, j):
    p, q, _, core = place()
    tile = RING * ((p + i) % RING) + (q + j) % RING
    return (tile % 2) ^ core, tile // 2


def call(kernel, out, *args, after=()):
    def run(*refs):
        kernel(*refs[: len(args)], *refs[len(args) + len(after) :])

    return pl.pallas_call(
        run,
        in_specs=[pl.BlockSpec(memory_space=pltpu.VMEM)] * len(args) + [pl.BlockSpec(memory_space=pl.ANY)] * len(after),
        out_shape=out,
        compiler_params=pltpu.CompilerParams(vmem_limit_bytes=24 * MIB),
        cost_estimate=pl.CostEstimate(flops=0, bytes_accessed=0, transcendentals=0),
    )(*args, *after)


def shape(dims, dtype):
    return jax.ShapeDtypeStruct(dims, dtype)


def along(first, k):
    pairs = []
    for y in range(RING):
        for x in range(RING):
            for z in range(DEPTH):
                for core in range(2):
                    if (core == 0) == first:
                        to = (y, (x + k) % RING)
                    else:
                        to = ((y + k) % RING, x)
                    t = z * 2 + core
                    pairs.append(((y * RING + x) * 2 * DEPTH + t, (to[0] * RING + to[1]) * 2 * DEPTH + t))
    return pairs


def send_p(a, k):
    return lax.ppermute(a, BOTH, along(True, k % RING))


def send_q(a, k):
    return lax.ppermute(a, BOTH, along(False, k % RING))


def send_core(a):
    return lax.ppermute(a, "tensor", [(i, i ^ 1) for i in range(2 * DEPTH)])


ORDER = (2, 1, 3)
CORES = [[z * 2 + c for z in range(DEPTH)] for c in range(2)]


def row_block(mine, other, i):
    tiles = []
    for j in range(RING):
        foreign, z = tile_at(i, j)
        tiles.append(jnp.where(foreign == 0, mine[z], other[z]))
    return jnp.concatenate(tiles, 0)


def join(*tiles, after=()):
    rows, columns = tiles[0].shape

    def kernel(*refs):
        for j, ref in enumerate(refs[:-1]):
            refs[-1][pl.ds(j * rows, rows)] = ref[...]

    return call(kernel, shape((len(tiles) * rows, columns), tiles[0].dtype), *tiles, after=after)


def gather_z(a):
    copies = jnp.broadcast_to(a, (DEPTH, *a.shape))
    mine = lax.all_to_all(copies, "tensor", 0, 0, tiled=True, axis_index_groups=CORES)
    return mine, send_core(mine)


def project(mine, other, gate_weight, up_weight, i, dtype, after=()):
    width, hidden = gate_weight.shape
    rows = RING * mine.shape[1]

    def kernel(mine_ref, other_ref, gate_ref, up_ref, out_ref):
        block = row_block(mine_ref, other_ref, i)
        out_ref[:, :hidden] = dot(block, gate_ref[...], (1, 0)).astype(dtype)
        out_ref[:, hidden:] = dot(block, up_ref[...], (1, 0)).astype(dtype)

    return call(kernel, shape((rows, 2 * hidden), dtype), mine, other, gate_weight, up_weight, after=after)


def grad_block(grads, i):
    core = place()[3]
    tiles = []
    for j in range(RING):
        foreign, z = tile_at(i, j)
        tiles.append(grads[2 * z + (foreign ^ core)])
    return jnp.concatenate(tiles, 0)


def project_grad(grads, down_weight, i, dtype):
    hidden, width = down_weight.shape
    rows = RING * grads.shape[1]

    def kernel(grads_ref, down_ref, out_ref):
        out_ref[...] = dot(grad_block(grads_ref, i), down_ref[...], (1, 1)).astype(dtype)

    return call(kernel, shape((rows, hidden), dtype), grads, down_weight)


def add_blocks(own, parts, after=()):
    rows, columns = own.shape
    tile = rows // RING

    def kernel(own_ref, a_ref, b_ref, c_ref, *outs):
        for j, out in enumerate(outs):
            at = pl.ds(j * tile, tile)
            out[...] = own_ref[at] + (a_ref[at].astype(F32) + b_ref[at].astype(F32) + c_ref[at].astype(F32))

    return call(kernel, [shape((tile, columns), F32)] * RING, own, *parts, after=after)


def spread(tiles):
    return [tiles[0]] + [send_q(tiles[j], j) for j in ORDER]


def activate(terms, after=()):
    rows, columns = terms[0].shape
    hidden = columns // 2

    def kernel(a, b, c, d, hidden_ref, up_factor, gate_factor):
        def total(at):
            return (a[:, at] + b[:, at]) + (c[:, at] + d[:, at])

        gate, up = total(pl.ds(0, hidden)), total(pl.ds(hidden, hidden))
        s = jax.nn.sigmoid(gate)
        activated = gate * s
        hidden_ref[...] = (activated * up).astype(BF16)
        up_factor[...] = activated
        gate_factor[...] = up * s * (1.0 + gate * (1.0 - s))

    outs = [shape((rows, hidden), BF16), shape((rows, hidden), F32), shape((rows, hidden), F32)]
    return call(kernel, outs, *terms, after=after)


def activate_grad(terms, up_factor, gate_factor):
    rows, hidden = up_factor.shape

    def kernel(a, b, c, d, up_ref, gate_ref, out_ref):
        hidden_grad = (a[...] + b[...]) + (c[...] + d[...])
        out_ref[:, :hidden] = (hidden_grad * gate_ref[...]).astype(BF16)
        out_ref[:, hidden:] = (hidden_grad * up_ref[...]).astype(BF16)

    return call(kernel, shape((rows, 2 * hidden), BF16), *terms, up_factor, gate_factor)


def gather_q(tile):
    return [tile] + [send_q(tile, -j) for j in range(1, RING)]


def gather_p(block):
    return [block] + [send_p(block, -i) for i in range(1, RING)]


def store_tile(mine, other, foreign, at, part):
    @pl.when(foreign == 0)
    def _():
        mine[at] = part

    @pl.when(foreign == 1)
    def _():
        other[at] = part


def store_tiles(mine, other, i, result):
    tile = mine.shape[1]
    for j in range(RING):
        store_tile(mine, other, *tile_at(i, j), result[j * tile : (j + 1) * tile])


def back(blocks, weights, after=()):
    hidden, width = weights.shape
    rows = blocks[0].shape[0]

    def kernel(a, b, c, d, weights_ref, mine, other):
        for i, block in enumerate((a, b, c, d)):
            store_tiles(mine, other, i, dot(block[...], weights_ref[...], (1, 0)))

    half = shape((DEPTH, rows // RING, width), F32)
    return call(kernel, [half, half], *blocks, weights, after=after)


def back_hidden(blocks, weights, after=()):
    width = weights.shape[1]
    rows = blocks[0].shape[0]
    tile = rows // RING

    def kernel(a, b, c, d, weights_ref, out):
        for i, block in enumerate((a, b, c, d)):
            result = dot(block[...], weights_ref[...], (1, 0))
            for j in range(RING):
                foreign, z = tile_at(i, j)
                out[z, pl.ds(pl.multiple_of(foreign * tile, tile), tile)] = result[j * tile : (j + 1) * tile]

    return call(kernel, shape((DEPTH, 2 * tile, width), F32), *blocks, weights, after=after)


def transposed(gate_weight, up_weight):
    width, hidden = gate_weight.shape

    def kernel(gate_ref, up_ref, out_ref):
        out_ref[:hidden] = gate_ref[...].T
        out_ref[hidden:] = up_ref[...].T

    return call(kernel, shape((2 * hidden, width), BF16), gate_weight, up_weight)


def reduce_z(mine, other, done):
    arrived = send_core(other)
    depth, rows, width = mine.shape

    def split(mine_ref, arrived_ref, own, out):
        own[...] = mine_ref[place()[2]] + arrived_ref[place()[2]]
        for k in range(depth):
            out[k] = (mine_ref[k] + arrived_ref[k]).astype(BF16)

    own, parts = call(split, [shape((rows, width), F32), shape(mine.shape, BF16)], mine, arrived)
    parts = lax.all_to_all(parts, "tensor", 0, 0, tiled=True, axis_index_groups=CORES)

    def add(own_ref, parts_ref, done_ref, more_ref, out, done_out):
        total = own_ref[...]
        for k in range(depth):
            total += jnp.where(place()[2] == k, 0.0, parts_ref[k].astype(F32))
        out[...] = total.astype(BF16)
        done_out[...] = (done_ref[...] + more_ref[...]).astype(BF16)

    return call(add, [shape((rows, width), BF16)] * 2, own, parts, *done)


def hidden_weight_grad(blocks, grads, factor):
    rows, hidden = blocks[0].shape
    width = grads.shape[2]

    def kernel(a, b, c, d, grads_ref, out_ref):
        for i, block in enumerate((a, b, c, d)):
            part = dot(block[...], grad_block(grads_ref, i), (0, 0)) * factor
            if i == 0:
                out_ref[...] = part
            else:
                out_ref[...] += part

    return call(
        kernel, shape((hidden, width), F32), *blocks, grads
    )


def token_weight_grads(blocks, mine, other, factor):
    rows, hidden = blocks[0].shape[0], blocks[0].shape[1] // 2
    width = mine.shape[2]

    def kernel(a, b, c, d, mine_ref, other_ref, gate_ref, up_ref):
        for i, block in enumerate((a, b, c, d)):
            tokens = row_block(mine_ref, other_ref, i)
            gate = dot(tokens, block[:, :hidden], (0, 0)) * factor
            up = dot(tokens, block[:, hidden:], (0, 0)) * factor
            if i == 0:
                gate_ref[...] = gate
                up_ref[...] = up
            else:
                gate_ref[...] += gate
                up_ref[...] += up

    out = shape((width, hidden), F32)
    return call(kernel, [out, out], *blocks, mine, other)


def body(tokens, gate_weight, up_weight, down_weight, out_grad):
    shard, width = tokens.shape
    rows = shard * 2 * DEPTH
    factor = 1.0 / math.sqrt(rows)

    rows_of = gather_z(tokens)
    grads = lax.all_gather(out_grad, "tensor", axis=0)
    blocks = {i: project(*rows_of, gate_weight, up_weight, i, BF16) for i in ORDER}
    blocks[0] = project(*rows_of, gate_weight, up_weight, 0, F32, after=[grads])
    grad_blocks = {i: project_grad(grads, down_weight, i, BF16 if i else F32) for i in (*ORDER, 0)}

    sent = [grad_blocks[i] for i in ORDER]
    tiles = add_blocks(blocks[0], [send_p(blocks[i], i) for i in ORDER], after=sent)
    grad_tiles = add_blocks(grad_blocks[0], [send_p(grad_blocks[i], i) for i in ORDER])
    hidden, up_factor, gate_factor = activate(spread(tiles), after=grad_tiles[:1])
    near = gather_q(hidden)
    grad_terms = spread(grad_tiles)
    grad_block = join(*gather_q(activate_grad(grad_terms, up_factor, gate_factor)))
    hidden_blocks = gather_p(join(*near, after=grad_terms[1:]))
    grad_blocks = gather_p(grad_block)

    partial = back_hidden(hidden_blocks, down_weight, after=[grad_block])
    down_weight_grad = hidden_weight_grad(hidden_blocks, grads, factor)
    partial = partial.reshape(rows, width)
    both = lax.psum_scatter(partial, "tensor", scatter_dimension=0, tiled=True, axis_index_groups=CORES)
    done = [both[:shard], send_core(both[shard:])]
    input_grad, ffn_output = reduce_z(*back(grad_blocks, transposed(gate_weight, up_weight), after=[down_weight_grad]), done)
    gate_weight_grad, up_weight_grad = token_weight_grads(grad_blocks, *rows_of, factor)
    return ffn_output, input_grad, gate_weight_grad, up_weight_grad, down_weight_grad


def solution(mesh):
    return jax.shard_map(
        body,
        mesh=mesh,
        in_specs=(
            P("tensor", "dp"),
            P("dp", "tensor"),
            P("dp", "tensor"),
            P("tensor", "dp"),
            P("tensor", "dp"),
        ),
        out_specs=(
            P("tensor", "dp"),
            P("tensor", "dp"),
            P("dp", "tensor"),
            P("dp", "tensor"),
            P("tensor", "dp"),
        ),
        check_vma=False,
    )
```

```python
import functools
import math

import jax
import jax.numpy as jnp
from jax import lax
from jax.experimental import pallas as pl
from jax.experimental.pallas import tpu as pltpu
from jax.sharding import PartitionSpec as P

MIB = 1024 * 1024
BF16 = jnp.bfloat16
F32 = jnp.float32
BOTH = ("dp", "tensor")
RING = 4
DEPTH = 8


def dot(a, b, contract):
    return lax.dot_general(a, b, ((contract[:1], contract[1:]), ((), ())), preferred_element_type=F32)


def place():
    dp, tensor = lax.axis_index("dp"), lax.axis_index("tensor")
    y, x, z, core = dp // RING, dp % RING, tensor // 2, tensor % 2
    return jnp.where(core == 0, x, y), jnp.where(core == 0, y, x), z, core


def tile_at(i, j):
    p, q, _, core = place()
    tile = RING * ((p + i) % RING) + (q + j) % RING
    return (tile % 2) ^ core, tile // 2


def call(kernel, out, *args, after=()):
    def run(*refs):
        kernel(*refs[: len(args)], *refs[len(args) + len(after) :])

    return pl.pallas_call(
        run,
        in_specs=[pl.BlockSpec(memory_space=pltpu.VMEM)] * len(args) + [pl.BlockSpec(memory_space=pl.ANY)] * len(after),
        out_shape=out,
        compiler_params=pltpu.CompilerParams(vmem_limit_bytes=24 * MIB),
        cost_estimate=pl.CostEstimate(flops=0, bytes_accessed=0, transcendentals=0),
    )(*args, *after)


def shape(dims, dtype):
    return jax.ShapeDtypeStruct(dims, dtype)


MARK = shape((8, 128), F32)


def along(first, k):
    pairs = []
    for y in range(RING):
        for x in range(RING):
            for z in range(DEPTH):
                for core in range(2):
                    if (core == 0) == first:
                        to = (y, (x + k) % RING)
                    else:
                        to = ((y + k) % RING, x)
                    t = z * 2 + core
                    pairs.append(((y * RING + x) * 2 * DEPTH + t, (to[0] * RING + to[1]) * 2 * DEPTH + t))
    return pairs


def send_p(a, k):
    return lax.ppermute(a, BOTH, along(True, k % RING))


def send_q(a, k):
    return lax.ppermute(a, BOTH, along(False, k % RING))


def send_core(a):
    return lax.ppermute(a, "tensor", [(i, i ^ 1) for i in range(2 * DEPTH)])


ORDER = (2, 1, 3)
CORES = [[z * 2 + c for z in range(DEPTH)] for c in range(2)]


def row_block(mine, other, i):
    tiles = []
    for j in range(RING):
        foreign, z = tile_at(i, j)
        tiles.append(jnp.where(foreign == 0, mine[z], other[z]))
    return jnp.concatenate(tiles, 0)


def join(*tiles, after=()):
    rows, columns = tiles[0].shape

    def kernel(*refs):
        for j, ref in enumerate(refs[:-1]):
            refs[-1][pl.ds(j * rows, rows)] = ref[...]

    return call(kernel, shape((len(tiles) * rows, columns), tiles[0].dtype), *tiles, after=after)


def gather_z(a):
    copies = jnp.broadcast_to(a, (DEPTH, *a.shape))
    mine = lax.all_to_all(copies, "tensor", 0, 0, tiled=True, axis_index_groups=CORES)
    return mine, send_core(mine)


def project(mine, other, gate_weight, up_weight, i, dtype, after=()):
    width, hidden = gate_weight.shape
    rows = RING * mine.shape[1]

    def kernel(mine_ref, other_ref, gate_ref, up_ref, out_ref):
        block = row_block(mine_ref, other_ref, i)
        out_ref[:, :hidden] = dot(block, gate_ref[...], (1, 0)).astype(dtype)
        out_ref[:, hidden:] = dot(block, up_ref[...], (1, 0)).astype(dtype)

    return call(kernel, shape((rows, 2 * hidden), dtype), mine, other, gate_weight, up_weight, after=after)


def grad_block(grads, i):
    core = place()[3]
    tiles = []
    for j in range(RING):
        foreign, z = tile_at(i, j)
        tiles.append(grads[2 * z + (foreign ^ core)])
    return jnp.concatenate(tiles, 0)


def project_grad(grads, down_weight, i, dtype):
    hidden, width = down_weight.shape
    rows = RING * grads.shape[1]

    def kernel(grads_ref, down_ref, out_ref):
        out_ref[...] = dot(grad_block(grads_ref, i), down_ref[...], (1, 1)).astype(dtype)

    return call(kernel, shape((rows, hidden), dtype), grads, down_weight)


def add_blocks(own, parts, after=()):
    rows, columns = own.shape
    tile = rows // RING

    def kernel(own_ref, a_ref, b_ref, c_ref, *outs):
        for j, out in enumerate(outs):
            at = pl.ds(j * tile, tile)
            out[...] = own_ref[at] + (a_ref[at].astype(F32) + b_ref[at].astype(F32) + c_ref[at].astype(F32))

    return call(kernel, [shape((tile, columns), F32)] * RING, own, *parts, after=after)


def spread(tiles):
    return [tiles[0]] + [send_q(tiles[j], j) for j in ORDER]


def activate(terms, after=()):
    rows, columns = terms[0].shape
    hidden = columns // 2

    def kernel(a, b, c, d, hidden_ref, up_factor, gate_factor):
        def total(at):
            return (a[:, at] + b[:, at]) + (c[:, at] + d[:, at])

        gate, up = total(pl.ds(0, hidden)), total(pl.ds(hidden, hidden))
        s = jax.nn.sigmoid(gate)
        activated = gate * s
        hidden_ref[...] = (activated * up).astype(BF16)
        up_factor[...] = activated
        gate_factor[...] = up * s * (1.0 + gate * (1.0 - s))

    outs = [shape((rows, hidden), BF16), shape((rows, hidden), F32), shape((rows, hidden), F32)]
    return call(kernel, outs, *terms, after=after)


def activate_grad(terms, up_factor, gate_factor):
    rows, hidden = up_factor.shape

    def kernel(a, b, c, d, up_ref, gate_ref, out_ref):
        hidden_grad = (a[...] + b[...]) + (c[...] + d[...])
        out_ref[:, :hidden] = (hidden_grad * gate_ref[...]).astype(BF16)
        out_ref[:, hidden:] = (hidden_grad * up_ref[...]).astype(BF16)

    return call(kernel, shape((rows, 2 * hidden), BF16), *terms, up_factor, gate_factor)


def gather_q(tile):
    return [tile] + [send_q(tile, -j) for j in range(1, RING)]


def gather_p(block):
    return [block] + [send_p(block, -i) for i in range(1, RING)]


def store_tile(mine, other, foreign, at, part):
    @pl.when(foreign == 0)
    def _():
        mine[at] = part

    @pl.when(foreign == 1)
    def _():
        other[at] = part


def store_tiles(mine, other, i, result):
    tile = mine.shape[1]
    for j in range(RING):
        store_tile(mine, other, *tile_at(i, j), result[j * tile : (j + 1) * tile])


def back(blocks, weights, after=()):
    width = weights.shape[1]
    tile = blocks[0].shape[0] // RING

    def kernel(a, b, c, weights_ref, mine, other):
        for i, block in enumerate((a, b, c)):
            store_tiles(mine, other, i, dot(block[...], weights_ref[...], (1, 0)))
        store_tiles(mine, other, RING - 1, jnp.zeros((RING * tile, width), F32))

    half = shape((DEPTH, tile, width), F32)
    return call(kernel, [half, half], *blocks[:-1], weights, after=after)


def back_last(block, weights):
    width = weights.shape[1]
    tile = block.shape[0] // RING

    def kernel(block_ref, weights_ref, mine, other):
        result = dot(block_ref[...], weights_ref[...], (1, 0))
        for j in range(RING):
            foreign, z = tile_at(RING - 1, j)
            store_tile(mine, other, foreign, z % 2, result[j * tile : (j + 1) * tile])

    half = shape((2, tile, width), F32)
    return call(kernel, [half, half], block, weights)


def back_hidden(blocks, weights, after=()):
    width = weights.shape[1]
    rows = blocks[0].shape[0]
    tile = rows // RING

    def kernel(a, b, c, d, weights_ref, out):
        for i, block in enumerate((a, b, c, d)):
            result = dot(block[...], weights_ref[...], (1, 0))
            for j in range(RING):
                foreign, z = tile_at(i, j)
                out[z, pl.ds(pl.multiple_of(foreign * tile, tile), tile)] = result[j * tile : (j + 1) * tile]

    return call(kernel, shape((DEPTH, 2 * tile, width), F32), *blocks, weights, after=after)


def transposed(gate_weight, up_weight):
    width, hidden = gate_weight.shape

    def kernel(gate_ref, up_ref, out_ref):
        out_ref[:hidden] = gate_ref[...].T
        out_ref[hidden:] = up_ref[...].T

    return call(kernel, shape((2 * hidden, width), BF16), gate_weight, up_weight)


def reduce_z(first, last, done):
    (mine, other), (mine_last, other_last) = first, last
    arrived, arrived_last = send_core(other), send_core(other_last)
    depth, rows, width = mine.shape

    def split(mine_ref, arrived_ref, mine_last_ref, arrived_last_ref, own, out):
        p, q, z, _ = place()
        last_mine, last_arrived = (p + RING - 1) % RING, (q + RING - 1) % RING

        def total(k):
            a = jnp.where(k // 2 == last_mine, mine_last_ref[k % 2], mine_ref[k])
            return a + jnp.where(k // 2 == last_arrived, arrived_last_ref[k % 2], arrived_ref[k])

        own[...] = total(z)
        for k in range(depth):
            out[k] = total(k).astype(BF16)

    outs = [shape((rows, width), F32), shape(mine.shape, BF16)]
    own, parts = call(split, outs, mine, arrived, mine_last, arrived_last)
    parts = lax.all_to_all(parts, "tensor", 0, 0, tiled=True, axis_index_groups=CORES)

    def add(own_ref, parts_ref, done_ref, more_ref, out, done_out):
        total = own_ref[...]
        for k in range(depth):
            total += jnp.where(place()[2] == k, 0.0, parts_ref[k].astype(F32))
        out[...] = total.astype(BF16)
        done_out[...] = (done_ref[...] + more_ref[...]).astype(BF16)

    return call(add, [shape((rows, width), BF16)] * 2, own, parts, *done)


def hidden_weight_grad(blocks, grads, factor):
    rows, hidden = blocks[0].shape
    width = grads.shape[2]

    def kernel(a, b, c, d, grads_ref, out_ref, mark):
        mark[...] = jnp.zeros_like(mark)
        for i, block in enumerate((a, b, c, d)):
            part = dot(block[...], grad_block(grads_ref, i), (0, 0)) * factor
            if i == 0:
                out_ref[...] = part
            else:
                out_ref[...] += part

    return call(kernel, [shape((hidden, width), F32), MARK], *blocks, grads)


def token_weight_grads(blocks, mine, other, factor):
    rows, hidden = blocks[0].shape[0], blocks[0].shape[1] // 2
    width = mine.shape[2]

    def kernel(a, b, c, d, mine_ref, other_ref, gate_ref, up_ref, mark):
        mark[...] = jnp.zeros_like(mark)
        for i, block in enumerate((a, b, c, d)):
            tokens = row_block(mine_ref, other_ref, i)
            gate = dot(tokens, block[:, :hidden], (0, 0)) * factor
            up = dot(tokens, block[:, hidden:], (0, 0)) * factor
            if i == 0:
                gate_ref[...] = gate
                up_ref[...] = up
            else:
                gate_ref[...] += gate
                up_ref[...] += up

    out = shape((width, hidden), F32)
    return call(kernel, [out, out, MARK], *blocks, mine, other)


def halves(a, after):
    rows, columns = a.shape

    def kernel(a_ref, first, second):
        first[...] = a_ref[: rows // 2]
        second[...] = a_ref[rows // 2 :]

    return call(kernel, [shape((rows // 2, columns), a.dtype)] * 2, a, after=after)


def body(tokens, gate_weight, up_weight, down_weight, out_grad):
    shard, width = tokens.shape
    rows = shard * 2 * DEPTH
    factor = 1.0 / math.sqrt(rows)

    rows_of = gather_z(tokens)
    grads = lax.all_gather(out_grad, "tensor", axis=0)
    blocks = {i: project(*rows_of, gate_weight, up_weight, i, BF16) for i in ORDER}
    blocks[0] = project(*rows_of, gate_weight, up_weight, 0, F32, after=[grads])
    grad_blocks = {i: project_grad(grads, down_weight, i, BF16 if i else F32) for i in (*ORDER, 0)}

    sent = [grad_blocks[i] for i in ORDER]
    tiles = add_blocks(blocks[0], [send_p(blocks[i], i) for i in ORDER], after=sent)
    grad_tiles = add_blocks(grad_blocks[0], [send_p(grad_blocks[i], i) for i in ORDER])
    hidden, up_factor, gate_factor = activate(spread(tiles), after=grad_tiles[:1])
    near = gather_q(hidden)
    grad_terms = spread(grad_tiles)
    grad_block = join(*gather_q(activate_grad(grad_terms, up_factor, gate_factor)))
    hidden_blocks = gather_p(join(*near, after=grad_terms[1:]))
    grad_blocks = gather_p(grad_block)

    partial = back_hidden(hidden_blocks, down_weight, after=[grad_block])
    down_weight_grad, mark = hidden_weight_grad(hidden_blocks, grads, factor)
    partial = partial.reshape(rows, width)
    both = lax.psum_scatter(partial, "tensor", scatter_dimension=0, tiled=True, axis_index_groups=CORES)
    weights = transposed(gate_weight, up_weight)
    first = back(grad_blocks, weights, after=[mark])
    gate_weight_grad, up_weight_grad, mark = token_weight_grads(grad_blocks, *rows_of, factor)
    own, foreign = halves(both, after=[mark])
    done = [own, send_core(foreign)]
    input_grad, ffn_output = reduce_z(first, back_last(grad_blocks[-1], weights), done)
    return ffn_output, input_grad, gate_weight_grad, up_weight_grad, down_weight_grad


def solution(mesh):
    return jax.shard_map(
        body,
        mesh=mesh,
        in_specs=(
            P("tensor", "dp"),
            P("dp", "tensor"),
            P("dp", "tensor"),
            P("tensor", "dp"),
            P("tensor", "dp"),
        ),
        out_specs=(
            P("tensor", "dp"),
            P("tensor", "dp"),
            P("dp", "tensor"),
            P("dp", "tensor"),
            P("tensor", "dp"),
        ),
        check_vma=False,
    )
```

```python
import functools
import math

import jax
import jax.numpy as jnp
from jax import lax
from jax.experimental import pallas as pl
from jax.experimental.pallas import tpu as pltpu
from jax.sharding import PartitionSpec as P

MIB = 1024 * 1024
BF16 = jnp.bfloat16
F32 = jnp.float32
BOTH = ("dp", "tensor")
RING = 4
DEPTH = 8


def dot(a, b, contract):
    return lax.dot_general(a, b, ((contract[:1], contract[1:]), ((), ())), preferred_element_type=F32)


def place():
    dp, tensor = lax.axis_index("dp"), lax.axis_index("tensor")
    y, x, z, core = dp // RING, dp % RING, tensor // 2, tensor % 2
    return jnp.where(core == 0, x, y), jnp.where(core == 0, y, x), z, core


def tile_at(i, j):
    p, q, _, core = place()
    tile = RING * ((p + i) % RING) + (q + j) % RING
    return (tile % 2) ^ core, tile // 2


def call(kernel, out, *args, after=()):
    def run(*refs):
        kernel(*refs[: len(args)], *refs[len(args) + len(after) :])

    return pl.pallas_call(
        run,
        in_specs=[pl.BlockSpec(memory_space=pltpu.VMEM)] * len(args) + [pl.BlockSpec(memory_space=pl.ANY)] * len(after),
        out_shape=out,
        compiler_params=pltpu.CompilerParams(vmem_limit_bytes=24 * MIB),
        cost_estimate=pl.CostEstimate(flops=0, bytes_accessed=0, transcendentals=0),
    )(*args, *after)


def shape(dims, dtype):
    return jax.ShapeDtypeStruct(dims, dtype)


MARK = shape((8, 128), F32)


def along(first, k):
    pairs = []
    for y in range(RING):
        for x in range(RING):
            for z in range(DEPTH):
                for core in range(2):
                    if (core == 0) == first:
                        to = (y, (x + k) % RING)
                    else:
                        to = ((y + k) % RING, x)
                    t = z * 2 + core
                    pairs.append(((y * RING + x) * 2 * DEPTH + t, (to[0] * RING + to[1]) * 2 * DEPTH + t))
    return pairs


def send_p(a, k):
    return lax.ppermute(a, BOTH, along(True, k % RING))


def send_q(a, k):
    return lax.ppermute(a, BOTH, along(False, k % RING))


def send_core(a):
    return lax.ppermute(a, "tensor", [(i, i ^ 1) for i in range(2 * DEPTH)])


ORDER = (1, 3, 2)
CORES = [[z * 2 + c for z in range(DEPTH)] for c in range(2)]


def row_block(mine, other, i):
    tiles = []
    for j in range(RING):
        foreign, z = tile_at(i, j)
        tiles.append(jnp.where(foreign == 0, mine[z], other[z]))
    return jnp.concatenate(tiles, 0)


def join(*tiles, after=()):
    rows, columns = tiles[0].shape

    def kernel(*refs):
        for j, ref in enumerate(refs[:-1]):
            refs[-1][pl.ds(j * rows, rows)] = ref[...]

    return call(kernel, shape((len(tiles) * rows, columns), tiles[0].dtype), *tiles, after=after)


def gather_z(a):
    copies = jnp.broadcast_to(a, (DEPTH, *a.shape))
    mine = lax.all_to_all(copies, "tensor", 0, 0, tiled=True, axis_index_groups=CORES)
    return mine, send_core(mine)


def project(mine, other, gate_weight, up_weight, i, dtype, after=()):
    width, hidden = gate_weight.shape
    rows = RING * mine.shape[1]

    def kernel(mine_ref, other_ref, gate_ref, up_ref, out_ref):
        block = row_block(mine_ref, other_ref, i)
        out_ref[:, :hidden] = dot(block, gate_ref[...], (1, 0)).astype(dtype)
        out_ref[:, hidden:] = dot(block, up_ref[...], (1, 0)).astype(dtype)

    return call(kernel, shape((rows, 2 * hidden), dtype), mine, other, gate_weight, up_weight, after=after)


def grad_block(grads, i):
    core = place()[3]
    tiles = []
    for j in range(RING):
        foreign, z = tile_at(i, j)
        tiles.append(grads[2 * z + (foreign ^ core)])
    return jnp.concatenate(tiles, 0)


def project_grad(grads, down_weight, i, dtype):
    hidden, width = down_weight.shape
    rows = RING * grads.shape[1]

    def kernel(grads_ref, down_ref, out_ref):
        out_ref[...] = dot(grad_block(grads_ref, i), down_ref[...], (1, 1)).astype(dtype)

    return call(kernel, shape((rows, hidden), dtype), grads, down_weight)


def add_blocks(own, parts, after=()):
    rows, columns = own.shape
    tile = rows // RING

    def kernel(own_ref, a_ref, b_ref, c_ref, *outs):
        for j, out in enumerate(outs):
            at = pl.ds(j * tile, tile)
            out[...] = own_ref[at] + (a_ref[at].astype(F32) + b_ref[at].astype(F32) + c_ref[at].astype(F32))

    return call(kernel, [shape((tile, columns), F32)] * RING, own, *parts, after=after)


def spread(tiles):
    return [tiles[0]] + [send_q(tiles[j], j) for j in ORDER]


def activate(terms, after=()):
    rows, columns = terms[0].shape
    hidden = columns // 2

    def kernel(a, b, c, d, hidden_ref, up_factor, gate_factor):
        def total(at):
            return (a[:, at] + b[:, at]) + (c[:, at] + d[:, at])

        gate, up = total(pl.ds(0, hidden)), total(pl.ds(hidden, hidden))
        s = jax.nn.sigmoid(gate)
        activated = gate * s
        hidden_ref[...] = (activated * up).astype(BF16)
        up_factor[...] = activated
        gate_factor[...] = up * s * (1.0 + gate * (1.0 - s))

    outs = [shape((rows, hidden), BF16), shape((rows, hidden), F32), shape((rows, hidden), F32)]
    return call(kernel, outs, *terms, after=after)


def activate_grad(terms, up_factor, gate_factor):
    rows, hidden = up_factor.shape

    def kernel(a, b, c, d, up_ref, gate_ref, out_ref):
        hidden_grad = (a[...] + b[...]) + (c[...] + d[...])
        out_ref[:, :hidden] = (hidden_grad * gate_ref[...]).astype(BF16)
        out_ref[:, hidden:] = (hidden_grad * up_ref[...]).astype(BF16)

    return call(kernel, shape((rows, 2 * hidden), BF16), *terms, up_factor, gate_factor)


def gather_q(tile):
    return [tile] + [send_q(tile, -j) for j in range(1, RING)]


def gather_p(block):
    return [block] + [send_p(block, -i) for i in range(1, RING)]


def store_tile(mine, other, foreign, at, part):
    @pl.when(foreign == 0)
    def _():
        mine[at] = part

    @pl.when(foreign == 1)
    def _():
        other[at] = part


def store_tiles(mine, other, i, result):
    tile = mine.shape[1]
    for j in range(RING):
        store_tile(mine, other, *tile_at(i, j), result[j * tile : (j + 1) * tile])


def back(blocks, weights, after=()):
    width = weights.shape[1]
    tile = blocks[0].shape[0] // RING

    def kernel(a, b, c, weights_ref, mine, other):
        for i, block in enumerate((a, b, c)):
            store_tiles(mine, other, i, dot(block[...], weights_ref[...], (1, 0)))
        store_tiles(mine, other, RING - 1, jnp.zeros((RING * tile, width), F32))

    half = shape((DEPTH, tile, width), F32)
    return call(kernel, [half, half], *blocks[:-1], weights, after=after)


def back_last(block, weights):
    width = weights.shape[1]
    tile = block.shape[0] // RING

    def kernel(block_ref, weights_ref, mine, other):
        result = dot(block_ref[...], weights_ref[...], (1, 0))
        for j in range(RING):
            foreign, z = tile_at(RING - 1, j)
            store_tile(mine, other, foreign, z % 2, result[j * tile : (j + 1) * tile])

    half = shape((2, tile, width), F32)
    return call(kernel, [half, half], block, weights)


def back_hidden(blocks, weights, after=()):
    width = weights.shape[1]
    rows = blocks[0].shape[0]
    tile = rows // RING

    def kernel(a, b, c, d, weights_ref, out):
        for i, block in enumerate((a, b, c, d)):
            result = dot(block[...], weights_ref[...], (1, 0))
            for j in range(RING):
                foreign, z = tile_at(i, j)
                out[z, pl.ds(pl.multiple_of(foreign * tile, tile), tile)] = result[j * tile : (j + 1) * tile]

    return call(kernel, shape((DEPTH, 2 * tile, width), F32), *blocks, weights, after=after)


def transposed(gate_weight, up_weight):
    width, hidden = gate_weight.shape

    def kernel(gate_ref, up_ref, out_ref):
        out_ref[:hidden] = gate_ref[...].T
        out_ref[hidden:] = up_ref[...].T

    return call(kernel, shape((2 * hidden, width), BF16), gate_weight, up_weight)


def reduce_z(first, last, done):
    (mine, other), (mine_last, other_last) = first, last
    arrived, arrived_last = send_core(other), send_core(other_last)
    depth, rows, width = mine.shape

    def split(mine_ref, arrived_ref, mine_last_ref, arrived_last_ref, own, out):
        p, q, z, _ = place()
        last_mine, last_arrived = (p + RING - 1) % RING, (q + RING - 1) % RING

        def total(k):
            a = jnp.where(k // 2 == last_mine, mine_last_ref[k % 2], mine_ref[k])
            return a + jnp.where(k // 2 == last_arrived, arrived_last_ref[k % 2], arrived_ref[k])

        own[...] = total(z)
        for k in range(depth):
            out[k] = total(k).astype(BF16)

    outs = [shape((rows, width), F32), shape(mine.shape, BF16)]
    own, parts = call(split, outs, mine, arrived, mine_last, arrived_last)
    parts = lax.all_to_all(parts, "tensor", 0, 0, tiled=True, axis_index_groups=CORES)

    def add(own_ref, parts_ref, done_ref, more_ref, out, done_out):
        total = own_ref[...]
        for k in range(depth):
            total += jnp.where(place()[2] == k, 0.0, parts_ref[k].astype(F32))
        out[...] = total.astype(BF16)
        done_out[...] = (done_ref[...] + more_ref[...]).astype(BF16)

    return call(add, [shape((rows, width), BF16)] * 2, own, parts, *done)


def hidden_weight_grad(blocks, grads, factor):
    rows, hidden = blocks[0].shape
    width = grads.shape[2]

    def kernel(a, b, c, d, grads_ref, out_ref, mark):
        mark[...] = jnp.zeros_like(mark)
        for i, block in enumerate((a, b, c, d)):
            part = dot(block[...], grad_block(grads_ref, i), (0, 0)) * factor
            if i == 0:
                out_ref[...] = part
            else:
                out_ref[...] += part

    return call(kernel, [shape((hidden, width), F32), MARK], *blocks, grads)


def token_weight_grads(blocks, mine, other, factor):
    rows, hidden = blocks[0].shape[0], blocks[0].shape[1] // 2
    width = mine.shape[2]

    def kernel(a, b, c, d, mine_ref, other_ref, gate_ref, up_ref, mark):
        mark[...] = jnp.zeros_like(mark)
        for i, block in enumerate((a, b, c, d)):
            tokens = row_block(mine_ref, other_ref, i)
            gate = dot(tokens, block[:, :hidden], (0, 0)) * factor
            up = dot(tokens, block[:, hidden:], (0, 0)) * factor
            if i == 0:
                gate_ref[...] = gate
                up_ref[...] = up
            else:
                gate_ref[...] += gate
                up_ref[...] += up

    out = shape((width, hidden), F32)
    return call(kernel, [out, out, MARK], *blocks, mine, other)


def halves(a, after):
    rows, columns = a.shape

    def kernel(a_ref, first, second):
        first[...] = a_ref[: rows // 2]
        second[...] = a_ref[rows // 2 :]

    return call(kernel, [shape((rows // 2, columns), a.dtype)] * 2, a, after=after)


def body(tokens, gate_weight, up_weight, down_weight, out_grad):
    shard, width = tokens.shape
    rows = shard * 2 * DEPTH
    factor = 1.0 / math.sqrt(rows)

    rows_of = gather_z(tokens)
    grads = lax.all_gather(out_grad, "tensor", axis=0)
    blocks = {i: project(*rows_of, gate_weight, up_weight, i, BF16) for i in ORDER}
    blocks[0] = project(*rows_of, gate_weight, up_weight, 0, F32, after=[grads])
    grad_blocks = {i: project_grad(grads, down_weight, i, BF16 if i else F32) for i in (*ORDER, 0)}

    sent = [grad_blocks[i] for i in ORDER]
    tiles = add_blocks(blocks[0], [send_p(blocks[i], i) for i in ORDER], after=sent)
    grad_tiles = add_blocks(grad_blocks[0], [send_p(grad_blocks[i], i) for i in ORDER])
    hidden, up_factor, gate_factor = activate(spread(tiles), after=grad_tiles[:1])
    near = gather_q(hidden)
    grad_terms = spread(grad_tiles)
    grad_block = join(*gather_q(activate_grad(grad_terms, up_factor, gate_factor)))
    hidden_blocks = gather_p(join(*near, after=grad_terms[1:]))
    grad_blocks = gather_p(grad_block)

    partial = back_hidden(hidden_blocks, down_weight, after=[grad_block])
    down_weight_grad, mark = hidden_weight_grad(hidden_blocks, grads, factor)
    partial = partial.reshape(rows, width)
    both = lax.psum_scatter(partial, "tensor", scatter_dimension=0, tiled=True, axis_index_groups=CORES)
    weights = transposed(gate_weight, up_weight)
    first = back(grad_blocks, weights, after=[mark])
    gate_weight_grad, up_weight_grad, mark = token_weight_grads(grad_blocks, *rows_of, factor)
    own, foreign = halves(both, after=[mark])
    done = [own, send_core(foreign)]
    input_grad, ffn_output = reduce_z(first, back_last(grad_blocks[-1], weights), done)
    return ffn_output, input_grad, gate_weight_grad, up_weight_grad, down_weight_grad


def solution(mesh):
    return jax.shard_map(
        body,
        mesh=mesh,
        in_specs=(
            P("tensor", "dp"),
            P("dp", "tensor"),
            P("dp", "tensor"),
            P("tensor", "dp"),
            P("tensor", "dp"),
        ),
        out_specs=(
            P("tensor", "dp"),
            P("tensor", "dp"),
            P("dp", "tensor"),
            P("dp", "tensor"),
            P("tensor", "dp"),
        ),
        check_vma=False,
    )
```

```python
import functools
import math

import jax
import jax.numpy as jnp
from jax import lax
from jax.experimental import pallas as pl
from jax.experimental.pallas import tpu as pltpu
from jax.sharding import PartitionSpec as P

MIB = 1024 * 1024
BF16 = jnp.bfloat16
F32 = jnp.float32
BOTH = ("dp", "tensor")
RING = 4
DEPTH = 8


def dot(a, b, contract):
    return lax.dot_general(a, b, ((contract[:1], contract[1:]), ((), ())), preferred_element_type=F32)


def place():
    dp, tensor = lax.axis_index("dp"), lax.axis_index("tensor")
    y, x, z, core = dp // RING, dp % RING, tensor // 2, tensor % 2
    return jnp.where(core == 0, x, y), jnp.where(core == 0, y, x), z, core


def tile_at(i, j):
    p, q, _, core = place()
    tile = RING * ((p + i) % RING) + (q + j) % RING
    return (tile % 2) ^ core, tile // 2


def call(kernel, out, *args, after=()):
    def run(*refs):
        kernel(*refs[: len(args)], *refs[len(args) + len(after) :])

    return pl.pallas_call(
        run,
        in_specs=[pl.BlockSpec(memory_space=pltpu.VMEM)] * len(args) + [pl.BlockSpec(memory_space=pl.ANY)] * len(after),
        out_shape=out,
        compiler_params=pltpu.CompilerParams(vmem_limit_bytes=24 * MIB),
        cost_estimate=pl.CostEstimate(flops=0, bytes_accessed=0, transcendentals=0),
    )(*args, *after)


def shape(dims, dtype):
    return jax.ShapeDtypeStruct(dims, dtype)


MARK = shape((8, 128), F32)


def along(first, k):
    pairs = []
    for y in range(RING):
        for x in range(RING):
            for z in range(DEPTH):
                for core in range(2):
                    if (core == 0) == first:
                        to = (y, (x + k) % RING)
                    else:
                        to = ((y + k) % RING, x)
                    t = z * 2 + core
                    pairs.append(((y * RING + x) * 2 * DEPTH + t, (to[0] * RING + to[1]) * 2 * DEPTH + t))
    return pairs


def send_p(a, k):
    return lax.ppermute(a, BOTH, along(True, k % RING))


def send_q(a, k):
    return lax.ppermute(a, BOTH, along(False, k % RING))


def send_core(a):
    return lax.ppermute(a, "tensor", [(i, i ^ 1) for i in range(2 * DEPTH)])


ORDER = (1, 3, 2)
CORES = [[z * 2 + c for z in range(DEPTH)] for c in range(2)]


def row_block(mine, other, i):
    tiles = []
    for j in range(RING):
        foreign, z = tile_at(i, j)
        tiles.append(jnp.where(foreign == 0, mine[z], other[z]))
    return jnp.concatenate(tiles, 0)


def join(*tiles, after=()):
    rows, columns = tiles[0].shape

    def kernel(*refs):
        for j, ref in enumerate(refs[:-1]):
            refs[-1][pl.ds(j * rows, rows)] = ref[...]

    return call(kernel, shape((len(tiles) * rows, columns), tiles[0].dtype), *tiles, after=after)


def gather_z(a):
    copies = jnp.broadcast_to(a, (DEPTH, *a.shape))
    mine = lax.all_to_all(copies, "tensor", 0, 0, tiled=True, axis_index_groups=CORES)
    return mine, send_core(mine)


def project(mine, other, gate_weight, up_weight, i, dtype, after=()):
    width, hidden = gate_weight.shape
    rows = RING * mine.shape[1]

    def kernel(mine_ref, other_ref, gate_ref, up_ref, out_ref):
        block = row_block(mine_ref, other_ref, i)
        out_ref[:, :hidden] = dot(block, gate_ref[...], (1, 0)).astype(dtype)
        out_ref[:, hidden:] = dot(block, up_ref[...], (1, 0)).astype(dtype)

    return call(kernel, shape((rows, 2 * hidden), dtype), mine, other, gate_weight, up_weight, after=after)


def grad_block(grads, i):
    core = place()[3]
    tiles = []
    for j in range(RING):
        foreign, z = tile_at(i, j)
        tiles.append(grads[2 * z + (foreign ^ core)])
    return jnp.concatenate(tiles, 0)


def project_grad(grads, down_weight, i, dtype):
    hidden, width = down_weight.shape
    rows = RING * grads.shape[1]

    def kernel(grads_ref, down_ref, out_ref):
        out_ref[...] = dot(grad_block(grads_ref, i), down_ref[...], (1, 1)).astype(dtype)

    return call(kernel, shape((rows, hidden), dtype), grads, down_weight)


def add_blocks(own, parts, after=()):
    rows, columns = own.shape
    tile = rows // RING

    def kernel(own_ref, a_ref, b_ref, c_ref, *outs):
        for j, out in enumerate(outs):
            at = pl.ds(j * tile, tile)
            out[...] = own_ref[at] + (a_ref[at].astype(F32) + b_ref[at].astype(F32) + c_ref[at].astype(F32))

    return call(kernel, [shape((tile, columns), F32)] * RING, own, *parts, after=after)


def spread(tiles):
    return [tiles[0]] + [send_q(tiles[j], j) for j in ORDER]


def activate(terms, after=()):
    rows, columns = terms[0].shape
    hidden = columns // 2

    def kernel(a, b, c, d, hidden_ref, up_factor, gate_factor):
        def total(at):
            return (a[:, at] + b[:, at]) + (c[:, at] + d[:, at])

        gate, up = total(pl.ds(0, hidden)), total(pl.ds(hidden, hidden))
        s = jax.nn.sigmoid(gate)
        activated = gate * s
        hidden_ref[...] = (activated * up).astype(BF16)
        up_factor[...] = activated
        gate_factor[...] = up * s * (1.0 + gate * (1.0 - s))

    outs = [shape((rows, hidden), BF16), shape((rows, hidden), F32), shape((rows, hidden), F32)]
    return call(kernel, outs, *terms, after=after)


def activate_grad(terms, up_factor, gate_factor):
    rows, hidden = up_factor.shape

    def kernel(a, b, c, d, up_ref, gate_ref, out_ref):
        hidden_grad = (a[...] + b[...]) + (c[...] + d[...])
        out_ref[:, :hidden] = (hidden_grad * gate_ref[...]).astype(BF16)
        out_ref[:, hidden:] = (hidden_grad * up_ref[...]).astype(BF16)

    return call(kernel, shape((rows, 2 * hidden), BF16), *terms, up_factor, gate_factor)


def gather_q(tile):
    return [tile] + [send_q(tile, -j) for j in range(1, RING)]


def gather_p(block):
    return [block] + [send_p(block, -i) for i in range(1, RING)]


def store_tile(mine, other, foreign, at, part):
    @pl.when(foreign == 0)
    def _():
        mine[at] = part

    @pl.when(foreign == 1)
    def _():
        other[at] = part


def store_tiles(mine, other, i, result):
    tile = mine.shape[1]
    for j in range(RING):
        store_tile(mine, other, *tile_at(i, j), result[j * tile : (j + 1) * tile])


def back(blocks, weights, after=()):
    width = weights.shape[1]
    tile = blocks[0].shape[0] // RING
    *early, late = ORDER

    def kernel(a, b, c, weights_ref, mine, other):
        for i, block in zip((0, *early), (a, b, c)):
            store_tiles(mine, other, i, dot(block[...], weights_ref[...], (1, 0)))
        store_tiles(mine, other, late, jnp.zeros((RING * tile, width), F32))

    half = shape((DEPTH, tile, width), F32)
    return call(kernel, [half, half], *(blocks[i] for i in (0, *early)), weights, after=after)


def back_last(block, weights):
    width = weights.shape[1]
    tile = block.shape[0] // RING

    def kernel(block_ref, weights_ref, mine, other):
        result = dot(block_ref[...], weights_ref[...], (1, 0))
        for j in range(RING):
            foreign, z = tile_at(ORDER[-1], j)
            store_tile(mine, other, foreign, z % 2, result[j * tile : (j + 1) * tile])

    half = shape((2, tile, width), F32)
    return call(kernel, [half, half], block, weights)


def back_hidden(blocks, weights, after=()):
    width = weights.shape[1]
    rows = blocks[0].shape[0]
    tile = rows // RING

    def kernel(a, b, c, d, weights_ref, out):
        for i, block in enumerate((a, b, c, d)):
            result = dot(block[...], weights_ref[...], (1, 0))
            for j in range(RING):
                foreign, z = tile_at(i, j)
                out[z, pl.ds(pl.multiple_of(foreign * tile, tile), tile)] = result[j * tile : (j + 1) * tile]

    return call(kernel, shape((DEPTH, 2 * tile, width), F32), *blocks, weights, after=after)


def transposed(gate_weight, up_weight):
    width, hidden = gate_weight.shape

    def kernel(gate_ref, up_ref, out_ref):
        out_ref[:hidden] = gate_ref[...].T
        out_ref[hidden:] = up_ref[...].T

    return call(kernel, shape((2 * hidden, width), BF16), gate_weight, up_weight)


def reduce_z(first, last, done):
    (mine, other), (mine_last, other_last) = first, last
    arrived, arrived_last = send_core(other), send_core(other_last)
    depth, rows, width = mine.shape

    def split(mine_ref, arrived_ref, mine_last_ref, arrived_last_ref, own, out):
        p, q, z, _ = place()
        last_mine, last_arrived = (p + ORDER[-1]) % RING, (q + ORDER[-1]) % RING

        def total(k):
            a = jnp.where(k // 2 == last_mine, mine_last_ref[k % 2], mine_ref[k])
            return a + jnp.where(k // 2 == last_arrived, arrived_last_ref[k % 2], arrived_ref[k])

        own[...] = total(z)
        for k in range(depth):
            out[k] = total(k).astype(BF16)

    outs = [shape((rows, width), F32), shape(mine.shape, BF16)]
    own, parts = call(split, outs, mine, arrived, mine_last, arrived_last)
    parts = lax.all_to_all(parts, "tensor", 0, 0, tiled=True, axis_index_groups=CORES)

    def add(own_ref, parts_ref, done_ref, more_ref, out, done_out):
        total = own_ref[...]
        for k in range(depth):
            total += jnp.where(place()[2] == k, 0.0, parts_ref[k].astype(F32))
        out[...] = total.astype(BF16)
        done_out[...] = (done_ref[...] + more_ref[...]).astype(BF16)

    return call(add, [shape((rows, width), BF16)] * 2, own, parts, *done)


def hidden_weight_grad(blocks, grads, factor):
    rows, hidden = blocks[0].shape
    width = grads.shape[2]

    def kernel(a, b, c, d, grads_ref, out_ref, mark):
        mark[...] = jnp.zeros_like(mark)
        for i, block in enumerate((a, b, c, d)):
            part = dot(block[...], grad_block(grads_ref, i), (0, 0)) * factor
            if i == 0:
                out_ref[...] = part
            else:
                out_ref[...] += part

    return call(kernel, [shape((hidden, width), F32), MARK], *blocks, grads)


def token_weight_grads(blocks, mine, other, factor):
    rows, hidden = blocks[0].shape[0], blocks[0].shape[1] // 2
    width = mine.shape[2]

    def kernel(a, b, c, d, mine_ref, other_ref, gate_ref, up_ref, mark):
        mark[...] = jnp.zeros_like(mark)
        for i, block in enumerate((a, b, c, d)):
            tokens = row_block(mine_ref, other_ref, i)
            gate = dot(tokens, block[:, :hidden], (0, 0)) * factor
            up = dot(tokens, block[:, hidden:], (0, 0)) * factor
            if i == 0:
                gate_ref[...] = gate
                up_ref[...] = up
            else:
                gate_ref[...] += gate
                up_ref[...] += up

    out = shape((width, hidden), F32)
    return call(kernel, [out, out, MARK], *blocks, mine, other)


def halves(a, after):
    rows, columns = a.shape

    def kernel(a_ref, first, second):
        first[...] = a_ref[: rows // 2]
        second[...] = a_ref[rows // 2 :]

    return call(kernel, [shape((rows // 2, columns), a.dtype)] * 2, a, after=after)


def body(tokens, gate_weight, up_weight, down_weight, out_grad):
    shard, width = tokens.shape
    rows = shard * 2 * DEPTH
    factor = 1.0 / math.sqrt(rows)

    rows_of = gather_z(tokens)
    grads = lax.all_gather(out_grad, "tensor", axis=0)
    blocks = {i: project(*rows_of, gate_weight, up_weight, i, BF16) for i in ORDER}
    blocks[0] = project(*rows_of, gate_weight, up_weight, 0, F32, after=[grads])
    grad_blocks = {i: project_grad(grads, down_weight, i, BF16 if i else F32) for i in (*ORDER, 0)}

    sent = [grad_blocks[i] for i in ORDER]
    tiles = add_blocks(blocks[0], [send_p(blocks[i], i) for i in ORDER], after=sent)
    grad_tiles = add_blocks(grad_blocks[0], [send_p(grad_blocks[i], i) for i in ORDER])
    hidden, up_factor, gate_factor = activate(spread(tiles), after=grad_tiles[:1])
    near = gather_q(hidden)
    grad_terms = spread(grad_tiles)
    grad_block = join(*gather_q(activate_grad(grad_terms, up_factor, gate_factor)))
    hidden_blocks = gather_p(join(*near, after=grad_terms[1:]))
    grad_blocks = gather_p(grad_block)

    partial = back_hidden(hidden_blocks, down_weight, after=[grad_block])
    down_weight_grad, mark = hidden_weight_grad(hidden_blocks, grads, factor)
    partial = partial.reshape(rows, width)
    both = lax.psum_scatter(partial, "tensor", scatter_dimension=0, tiled=True, axis_index_groups=CORES)
    weights = transposed(gate_weight, up_weight)
    first = back(grad_blocks, weights, after=[mark])
    gate_weight_grad, up_weight_grad, mark = token_weight_grads(grad_blocks, *rows_of, factor)
    own, foreign = halves(both, after=[mark])
    done = [own, send_core(foreign)]
    input_grad, ffn_output = reduce_z(first, back_last(grad_blocks[ORDER[-1]], weights), done)
    return ffn_output, input_grad, gate_weight_grad, up_weight_grad, down_weight_grad


def solution(mesh):
    return jax.shard_map(
        body,
        mesh=mesh,
        in_specs=(
            P("tensor", "dp"),
            P("dp", "tensor"),
            P("dp", "tensor"),
            P("tensor", "dp"),
            P("tensor", "dp"),
        ),
        out_specs=(
            P("tensor", "dp"),
            P("tensor", "dp"),
            P("dp", "tensor"),
            P("dp", "tensor"),
            P("tensor", "dp"),
        ),
        check_vma=False,
    )
```
